128 devices in a mesh: row: 8 (over x, core), col: 16 (over z, y).
Axes of the slice: x: 4, y: 4, z: 4, core: 2. Of those that a mesh axis runs over, the one named last changes fastest.
Arguments:
- hinverse: float32 [6, 8, 256, 3, 16, 256], P(None, 'row', None, None, 'col'), as said below
- pruned: int32 [2, 256], replicated, may hold values from 0 to 12287, as said below
- weights: float32 [6144, 3, 16, 256], P('row', None, 'col'), may hold values from -6 to 6
Outputs:
- hinverse_out: float32 [6, 8, 256, 3, 16, 256], P(None, 'row', None, None, 'col')
- weights_out: float32 [6144, 3, 16, 256], P('row', None, 'col')
The draws below stay inside these ranges and needn't reach their ends.
Inputs may be any that keep to these rules, and one draw needn't show every extreme that they name: `pruned`: all 2 x 256 indices are distinct; 0 and 12287 occur. hinverse is symmetric positive definite.
All inputs are finite; a program needn't handle non-finite values.
Results may differ from the reference program's by a relative error of at most 0.00017.
Values sent between devices are 32-bit elements; how exact they have to be, the bound alone decides.
A program may use at most 128 MiB of HBM per device.

```python
import math
import jax
import jax.numpy as jnp
from jax import lax

M = 12288
TILE = 256
K = 256
ROUNDS = 2
R = 6144
TROW_DEV = 6
TCOL_DEV = 3
N_ROW = 8
N_COL = 16


def draw_hinverse(key, part):
    key = jax.random.fold_in(key, 11)
    key_scale = jax.random.fold_in(key, 0)
    key_base = jax.random.fold_in(key, 1)
    key_noise = jax.random.fold_in(key, 2)
    key_place = jax.random.fold_in(key, 4)
    spread = math.log(10.0)
    reach = 0.25
    scales = jnp.exp(jax.random.uniform(key_scale, (M,), jnp.float32, 0.0, spread))
    base = 1.5 + jax.random.uniform(key_base, (M,), jnp.float32)
    where = jax.random.uniform(key_place, (3, M), jnp.float32)
    distance = jnp.abs(where[0][:, None] - where[0][None, :])
    distance = distance + jnp.abs(where[1][:, None] - where[1][None, :])
    distance = distance + jnp.abs(where[2][:, None] - where[2][None, :])
    kernel = jnp.exp(distance * (-1.0 / reach))
    noise = jax.random.uniform(key_noise, (M, M), jnp.float32, -1.0, 1.0)
    noise = (noise + noise.T) * (0.35 / math.sqrt(2.0 * M))
    places = jnp.arange(M)
    eye = (places[:, None] == places[None, :]).astype(jnp.float32)
    root = jnp.sqrt(scales)
    full = root[:, None] * root[None, :] * (eye * base[:, None] + kernel + noise)
    return full.reshape(TROW_DEV, N_ROW, TILE, TCOL_DEV, N_COL, TILE)


def draw_pruned(key, part):
    key = jax.random.fold_in(key, 23)
    key_pick, key_order = jax.random.split(key)
    inner = jax.random.permutation(key_pick, M - 2)[:ROUNDS * K - 2] + 1
    values = jnp.concatenate([jnp.array([0, M - 1], jnp.int32), inner.astype(jnp.int32)])
    shuffle = jax.random.permutation(key_order, ROUNDS * K)
    return values[shuffle].reshape(ROUNDS, K).astype(jnp.int32)


def levels(rng, shape, cuts, smallest, largest):
    def one(position, shards_of):
        steps = jax.random.uniform(jax.random.fold_in(jax.random.fold_in(rng, 6), position), (shards_of,), jnp.float32, smallest / len(cuts), largest / len(cuts))
        return jnp.repeat(jnp.exp(steps), shape[position] // shards_of).reshape((-1,) + (1,) * (len(shape) - position - 1))

    gain = one(*cuts[0])
    for cut in cuts[1:]:
        gain = gain * one(*cut)
    return gain


def gaussian(own_key, shape, scale, bound, cuts=(), held_as=jnp.bfloat16):
    level = levels(own_key, shape, cuts, -0.22, 0.18) if cuts else 1.0
    result = jax.random.normal(own_key, shape, jnp.float32) * scale * level
    return jnp.minimum(jnp.maximum(result, -bound), bound).astype(held_as)


def setup_inputs(seed: int = 0) -> dict:
    key_list = jax.random.split(jax.random.key(seed), 4)
    hinverse = draw_hinverse(jax.random.fold_in(key_list[3], 71), 0)
    pruned = draw_pruned(jax.random.fold_in(key_list[3], 71), 0)
    weights = gaussian(key_list[2], (R, TCOL_DEV, N_COL, TILE), 1.0, 6.0, ((0, 8), (2, 16)), jnp.float32)
    return {"hinverse": hinverse, "pruned": pruned, "weights": weights}


def invert_block(block):
    factor = jnp.linalg.cholesky(block)
    eye = jnp.eye(block.shape[0], dtype=block.dtype)
    lower_inv = lax.linalg.triangular_solve(factor, eye, left_side=True, lower=True)
    return jnp.dot(lower_inv.T, lower_inv, precision=lax.Precision.HIGHEST)

def reference(hinverse, pruned, weights):
    order = hinverse.shape[0] * hinverse.shape[1] * hinverse.shape[2]
    matrix = hinverse.reshape(order, order)
    weight_rows = weights.reshape(weights.shape[0], order)
    for step in range(pruned.shape[0]):
        picked = pruned[step].astype(jnp.int32)
        columns = matrix[:, picked]
        panel = matrix[picked, :]
        inverse = invert_block(columns[picked, :])
        mixed = jnp.dot(inverse, panel, precision=lax.Precision.HIGHEST)
        matrix = matrix - jnp.dot(columns, mixed, precision=lax.Precision.HIGHEST)
        gains = jnp.dot(weight_rows[:, picked], inverse, precision=lax.Precision.HIGHEST)
        weight_rows = weight_rows - jnp.dot(gains, panel, precision=lax.Precision.HIGHEST)
        weight_rows = weight_rows.at[:, picked].set(0.0)
    return (matrix.reshape(hinverse.shape), weight_rows.reshape(weights.shape))
```

```python
import functools

import jax
import jax.numpy as jnp
from jax import lax
from jax.experimental import pallas as pl
from jax.experimental.pallas import tpu as pltpu
from jax.sharding import PartitionSpec as P

F = jnp.float32
B = jnp.bfloat16
MESH = pl.DeviceIdType.MESH
HIGHEST = lax.Precision.HIGHEST
NN = ((1,), (0,))
NT = ((1,), (1,))
TN = ((0,), (0,))
ANY = pl.BlockSpec(memory_space=pl.ANY)
VMEM = pl.BlockSpec(memory_space=pltpu.VMEM)
LIMIT = 56 * 2**20


def split3(x):
    hi = x.astype(B)
    rest = x - hi.astype(F)
    mid = rest.astype(B)
    return hi, mid, (rest - mid.astype(F)).astype(B)


def split2(x):
    hi = x.astype(B)
    return hi, (x - hi.astype(F)).astype(B)


def dot(a, b, dims):
    return lax.dot_general(a, b, (dims, ((), ())), preferred_element_type=F)


def pick(onehot, x, dims):
    hi, mid, lo = split3(x)
    return dot(onehot, lo, dims) + dot(onehot, mid, dims) + dot(onehot, hi, dims)


def dot3(a, b, dims):
    (ah, al), (bh, bl) = a, b
    return dot(al, bh, dims) + dot(ah, bl, dims) + dot(ah, bh, dims)


def local_place(p_ref, parts, index):
    p = jnp.concatenate([p_ref[0:1, :], p_ref[1:2, :]], axis=1)
    p = jnp.broadcast_to(p, (128, p.shape[1])).T
    tile = p >> 8
    return jnp.where(tile % parts == index, (tile // parts) * 256 + (p & 255), -1)


def onehot(place, start, width):
    lane = lax.broadcasted_iota(jnp.int32, place.shape, 1)
    blocks = [(place == lane + (start + 128 * q)).astype(F).astype(B) for q in range(width // 128)]
    return jnp.concatenate(blocks, axis=1)


def gather_kernel(h_hbm, w_hbm, p_ref, t_ref, wt_ref, hv, wv, sem):
    row = lax.axis_index("row")
    col = lax.axis_index("col")
    h_copies, w_copies = [], []
    for a in range(6):
        for b in range(3):
            copy = pltpu.make_async_copy(
                h_hbm.at[a, 0, :, b, 0, :], hv.at[pl.ds(256 * a, 256), pl.ds(256 * b, 256)], sem.at[3 * a + b]
            )
            copy.start()
            h_copies.append(copy)
    for b in range(3):
        copy = pltpu.make_async_copy(w_hbm.at[:, b, 0, :], wv.at[:, pl.ds(256 * b, 256)], sem.at[18 + b])
        copy.start()
        w_copies.append(copy)
    rows = local_place(p_ref, 8, row)
    cols = local_place(p_ref, 16, col)
    for a in range(6):
        for copy in h_copies[3 * a : 3 * a + 3]:
            copy.wait()
        part = pick(onehot(rows, 256 * a, 256), hv[256 * a : 256 * a + 256, :], NN)
        t_ref[...] = part if a == 0 else t_ref[...] + part
    for b in range(3):
        w_copies[b].wait()
        part = pick(onehot(cols, 256 * b, 256), wv[:, 256 * b : 256 * b + 256], NT)
        wt_ref[...] = part if b == 0 else wt_ref[...] + part


def gather(hinverse, pruned, weights):
    return pl.pallas_call(
        gather_kernel,
        out_shape=[jax.ShapeDtypeStruct((512, 768), F)] * 2,
        in_specs=[ANY, ANY, VMEM],
        out_specs=[VMEM, VMEM],
        scratch_shapes=[
            pltpu.VMEM((1536, 768), F),
            pltpu.VMEM((768, 768), F),
            pltpu.SemaphoreType.DMA((21,)),
        ],
        compiler_params=pltpu.CompilerParams(vmem_limit_bytes=LIMIT),
        name="gather",
    )(hinverse, weights, pruned)


class Links:
    def __init__(self, send, recv):
        self.send, self.recv, self.count, self.started = send, recv, 0, []

    def copy(self, src, dst, device):
        n = self.count
        self.count += 1
        made = pltpu.make_async_remote_copy(
            src_ref=src, dst_ref=dst, send_sem=self.send.at[n], recv_sem=self.recv.at[n], device_id=device, device_id_type=MESH
        )
        made.start()
        self.started.append(made)
        return made

    def drain(self):
        for made in self.started:
            made.wait_send()


class RingSum:
    def __init__(self, links, i, up, down, full, half, boxes):
        self.links, self.i, self.up, self.down = links, i, up, down
        self.full, self.half, self.boxes = full, half, boxes

    def far(self):
        left, right, _, _ = self.boxes
        j = (self.i + 2) % 4
        self.a = self.links.copy(self.half(j, 0), left, self.up)
        self.b = self.links.copy(self.half(j, 1), right, self.down)

    def near(self):
        left, right, left2, right2 = self.boxes
        up, down = (self.i + 1) % 4, (self.i + 3) % 4
        self.a.wait_recv()
        part = self.half(up, 0)
        part[...] = part[...] + left[...]
        self.a = self.links.copy(self.full(up), left2, self.up)
        self.b.wait_recv()
        part = self.half(down, 1)
        part[...] = part[...] + right[...]
        self.b = self.links.copy(self.full(down), right2, self.down)

    def finish(self):
        _, _, left2, right2 = self.boxes
        self.a.wait_recv()
        self.b.wait_recv()
        return self.full(self.i)[...] + left2[...] + right2[...]


class RingGather:
    def __init__(self, links, i, up, down, full, half):
        self.links, self.i, self.up, self.down = links, i, up, down
        self.full, self.half = full, half

    def own(self):
        mine = self.full(self.i)
        self.a = self.links.copy(mine, mine, self.up)
        self.b = self.links.copy(mine, mine, self.down)

    def forward(self):
        self.a.wait_recv()
        part = self.half((self.i + 3) % 4, 0)
        self.a = self.links.copy(part, part, self.up)
        self.b.wait_recv()
        part = self.half((self.i + 1) % 4, 1)
        self.b = self.links.copy(part, part, self.down)

    def finish(self):
        self.a.wait_recv()
        self.b.wait_recv()


def exchange_kernel(t_ref, wt_ref, p_ref, s_hbm, pan_hbm, y_hbm, w_hbm,
                    ra, xbox1, xbox2, wc, wboxf, wboxn, wbox2f, wbox2n, sm, srx, s, pan, y, w, send, recv, osem):
    row = lax.axis_index("row")
    col = lax.axis_index("col")
    x, k = row // 2, row % 2
    z, yy = col // 4, col % 4

    def dev(r, c):
        return {"row": r, "col": c}

    sibling = dev(2 * x + 1 - k, col)
    x_up, x_down = dev(2 * ((x + 1) % 4) + k, col), dev(2 * ((x + 3) % 4) + k, col)
    y_up, y_down = dev(row, 4 * z + (yy + 1) % 4), dev(row, 4 * z + (yy + 3) % 4)
    z_up, z_down = dev(row, (col + 4) % 16), dev(row, (col + 12) % 16)
    target = dev(col % 8, (1 - col // 8) * 8 + 4 * k + x)
    source = dev(2 * (col % 4) + (col % 8) // 4, row + 8 * (1 - col // 8))
    peers = [dev(row, (col + d) % 16) for d in range(1, 16)]

    barrier = pltpu.get_barrier_semaphore()
    greet = [sibling, x_up, x_down, target, source] + peers
    for device in greet:
        pl.semaphore_signal(barrier, inc=1, device_id=device, device_id_type=MESH)
    pl.semaphore_wait(barrier, len(greet))

    links = Links(send, recv)
    order = [(x + 2) % 4, (x + 1) % 4, (x + 3) % 4, x]
    halves = [links.copy(t_ref.at[4 * (1 - k) + j], ra.at[j], sibling) for j in order]

    sum_z0 = RingSum(links, z, z_up, z_down, lambda j: wt_ref.at[j, :, 0], lambda j, h: wt_ref.at[j, pl.ds(2 * h, 2), 0],
                     (wboxf.at[0], wboxf.at[1], wboxn.at[0], wboxn.at[1]))
    sum_y1 = RingSum(links, yy, y_up, y_down, lambda j: wt_ref.at[:, j, 1], lambda j, h: wt_ref.at[pl.ds(2 * h, 2), j, 1],
                     (wboxf.at[2], wboxf.at[3], wboxn.at[2], wboxn.at[3]))
    sum_y0 = RingSum(links, yy, y_up, y_down, lambda j: wc.at[0, j], lambda j, h: wc.at[0, j, pl.ds(8 * h, 8)],
                     (wbox2f.at[0], wbox2f.at[1], wbox2n.at[0], wbox2n.at[1]))
    sum_z1 = RingSum(links, z, z_up, z_down, lambda j: wc.at[1, j], lambda j, h: wc.at[1, j, pl.ds(8 * h, 8)],
                     (wbox2f.at[2], wbox2f.at[3], wbox2n.at[2], wbox2n.at[3]))
    sum_z0.far()
    sum_y1.far()

    sum_x = RingSum(links, x, x_up, x_down, lambda j: ra.at[j], lambda j, h: ra.at[j, pl.ds(32 * h, 32)],
                    (xbox1.at[0], xbox1.at[1], xbox2.at[0], xbox2.at[1]))
    for n, j in enumerate(order):
        halves[n].wait_recv()
        ra[j] = ra[j] + t_ref[4 * k + j]
        if n == 0:
            sum_x.far()
    sum_x.near()
    sum_z0.near()
    sum_y1.near()
    slot = 4 * k + x
    pan[slot] = sum_x.finish()
    moved = links.copy(pan.at[slot], y.at[target["col"]], target)
    pan_x = RingGather(links, x, x_up, x_down, lambda j: pan.at[4 * k + j], lambda j, h: pan.at[4 * k + j, pl.ds(32 * h, 32)])
    pan_x.own()

    cols = local_place(p_ref, 16, col)
    total = jnp.zeros((64, 512), F)
    for b in range(3):
        hi, mid, lo = split3(pan[slot, :, 256 * b : 256 * b + 256])
        hot = onehot(cols, 256 * b, 256)
        total = total + dot(lo, hot, NT) + dot(mid, hot, NT) + dot(hi, hot, NT)
    sm[0] = total[:, :256].reshape(8, 8, 256)
    sm[1] = total[:, 256:].reshape(8, 8, 256)

    def s_copy(ref_src, dst, d):
        return links.copy(ref_src, dst, peers[d - 1])

    a2a = []
    for d in range(1, 16):
        q = (col + d) % 16
        a2a.append(s_copy(sm.at[q % 2, q // 2], srx.at[d - 1], d))

    wc[0] = sum_z0.finish()
    wc[1] = sum_y1.finish()
    sum_y0.far()
    sum_z1.far()

    piece = sm[col % 2, col // 2]
    for d in range(1, 16):
        a2a[d - 1].wait_recv()
        piece = piece + srx[d - 1]
    own_s = s.at[col % 2, slot, pl.ds(pl.multiple_of(8 * (col // 2), 8), 8)]
    own_s[...] = piece
    spread = [s_copy(own_s, own_s, d) for d in range(1, 16)]

    sum_y0.near()
    sum_z1.near()

    moved.wait_recv()
    y_y0 = RingGather(links, yy, y_up, y_down, lambda j: y.at[4 * z + j, pl.ds(0, 32)], lambda j, h: y.at[4 * z + j, pl.ds(16 * h, 16)])
    y_z1 = RingGather(links, z, z_up, z_down, lambda j: y.at[4 * j + yy, pl.ds(32, 32)], lambda j, h: y.at[4 * j + yy, pl.ds(32 + 16 * h, 16)])
    yr = y.reshape(4, 4, 64, 768)
    y_z0 = RingGather(links, z, z_up, z_down, lambda j: yr.at[j, :, pl.ds(0, 32)], lambda j, h: yr.at[j, pl.ds(2 * h, 2), pl.ds(0, 32)])
    y_y1 = RingGather(links, yy, y_up, y_down, lambda j: yr.at[:, j, pl.ds(32, 32)], lambda j, h: yr.at[pl.ds(2 * h, 2), j, pl.ds(32, 32)])
    y_y0.own()
    y_z1.own()

    for copy in spread:
        copy.wait_recv()
    s_x = RingGather(links, x, x_up, x_down, lambda j: s.at[:, 4 * k + j], lambda j, h: s.at[h, 4 * k + j])
    s_x.own()
    pan_x.forward()
    s_x.forward()

    w[z, yy, 0] = sum_y0.finish()
    w[z, yy, 1] = sum_z1.finish()
    w_y0 = RingGather(links, yy, y_up, y_down, lambda j: w.at[z, j, 0], lambda j, h: w.at[z, j, 0, pl.ds(8 * h, 8)])
    w_z1 = RingGather(links, z, z_up, z_down, lambda j: w.at[j, yy, 1], lambda j, h: w.at[j, yy, 1, pl.ds(8 * h, 8)])
    w_z0 = RingGather(links, z, z_up, z_down, lambda j: w.at[j, :, 0], lambda j, h: w.at[j, pl.ds(2 * h, 2), 0])
    w_y1 = RingGather(links, yy, y_up, y_down, lambda j: w.at[:, j, 1], lambda j, h: w.at[pl.ds(2 * h, 2), j, 1])
    w_y0.own()
    w_z1.own()

    y_y0.forward()
    y_z1.forward()
    s_x.finish()
    mine_s = s.at[:, pl.ds(4 * k, 4)]
    swap_s = links.copy(mine_s, mine_s, sibling)
    w_y0.forward()
    w_z1.forward()
    pan_x.finish()
    mine = pan.at[pl.ds(4 * k, 4)]
    swap = links.copy(mine, mine, sibling)
    y_y0.finish()
    y_z0.own()
    y_z1.finish()
    y_y1.own()
    w_y0.finish()
    w_z0.own()
    w_z1.finish()
    w_y1.own()
    swap_s.wait_recv()
    swap.wait_recv()
    outs = [pltpu.make_async_copy(s, s_hbm, osem.at[0]), pltpu.make_async_copy(pan, pan_hbm, osem.at[1])]
    for copy in outs:
        copy.start()
    y_z0.forward()
    y_y1.forward()
    w_z0.forward()
    w_y1.forward()
    y_z0.finish()
    y_y1.finish()
    outs.append(pltpu.make_async_copy(y, y_hbm, osem.at[2]))
    outs[-1].start()
    w_z0.finish()
    w_y1.finish()
    outs.append(pltpu.make_async_copy(w, w_hbm, osem.at[3]))
    outs[-1].start()
    for copy in outs:
        copy.wait()
    links.drain()


COPIES = 104


def exchange(t, wt, pruned):
    return pl.pallas_call(
        exchange_kernel,
        out_shape=[
            jax.ShapeDtypeStruct((2, 8, 64, 256), F),
            jax.ShapeDtypeStruct((8, 64, 768), F),
            jax.ShapeDtypeStruct((16, 64, 768), F),
            jax.ShapeDtypeStruct((4, 4, 2, 16, 768), F),
        ],
        in_specs=[VMEM, VMEM, VMEM],
        out_specs=[ANY] * 4,
        scratch_shapes=[
            pltpu.VMEM((4, 64, 768), F),
            pltpu.VMEM((2, 32, 768), F),
            pltpu.VMEM((2, 64, 768), F),
            pltpu.VMEM((2, 4, 16, 768), F),
            pltpu.VMEM((4, 2, 16, 768), F),
            pltpu.VMEM((4, 4, 16, 768), F),
            pltpu.VMEM((4, 8, 768), F),
            pltpu.VMEM((4, 16, 768), F),
            pltpu.VMEM((2, 8, 8, 256), F),
            pltpu.VMEM((15, 8, 256), F),
            pltpu.VMEM((2, 8, 64, 256), F),
            pltpu.VMEM((8, 64, 768), F),
            pltpu.VMEM((16, 64, 768), F),
            pltpu.VMEM((4, 4, 2, 16, 768), F),
            pltpu.SemaphoreType.DMA((COPIES,)),
            pltpu.SemaphoreType.DMA((COPIES,)),
            pltpu.SemaphoreType.DMA((4,)),
        ],
        compiler_params=pltpu.CompilerParams(vmem_limit_bytes=LIMIT, collective_id=0, has_side_effects=True),
        name="exchange",
    )(t.reshape(8, 64, 768), wt.reshape(4, 4, 2, 16, 768), pruned)


def sweep8(groups, m):
    n = 8 * len(groups)
    row = groups[m]
    sub = lax.broadcasted_iota(jnp.int32, (8, n), 0)
    lane = lax.broadcasted_iota(jnp.int32, (8, n), 1)
    c = [jnp.broadcast_to(row[:, 8 * m + j : 8 * m + j + 1], (8, n)) for j in range(8)]
    for k in range(8):
        pivot = 1.0 / jnp.broadcast_to(c[k][k : k + 1, :], (8, n))
        at_k = sub == k
        ck = c[k]
        for j in range(8):
            if j != k:
                t = jnp.broadcast_to(c[j][k : k + 1, :], (8, n)) * pivot
                c[j] = jnp.where(at_k, t, c[j] - ck * t)
        c[k] = jnp.where(at_k, pivot, -(ck * pivot))
    inside = (lane >= 8 * m) & (lane < 8 * m + 8)
    row = jnp.where(inside, jnp.where(lane - 8 * m == sub, 1.0, 0.0), row)
    new = c[0] * jnp.broadcast_to(row[0:1, :], (8, n))
    for j in range(1, 8):
        new = new + c[j] * jnp.broadcast_to(row[j : j + 1, :], (8, n))
    spread = [jnp.broadcast_to(new[j : j + 1, :], (8, n)) for j in range(8)]
    out = []
    for i, group in enumerate(groups):
        if i == m:
            out.append(new)
            continue
        left = jnp.where(inside, 0.0, group)
        for j in range(8):
            left = left - jnp.broadcast_to(group[:, 8 * m + j : 8 * m + j + 1], (8, n)) * spread[j]
        out.append(left)
    return out


def invert128(block):
    groups = [block[8 * i : 8 * i + 8, :] for i in range(16)]
    for m in range(16):
        groups = sweep8(groups, m)
    return jnp.concatenate(groups, axis=0)


def fdot(a, b):
    return jnp.dot(a, b, precision=HIGHEST, preferred_element_type=F)


def invert_kernel(s_ref, x_ref):
    x_ref[:, :256] = s_ref[0]
    x_ref[:, 256:] = s_ref[1]
    square = x_ref[...]
    x_ref[...] = (square + square.T) * 0.5
    for k in range(4):
        here = slice(128 * k, 128 * k + 128)
        inverse = invert128(x_ref[here, here])
        row = fdot(inverse, x_ref[here, :])
        column = x_ref[:, here]
        x_ref[...] = x_ref[...] - fdot(column, row)
        x_ref[:, here] = -fdot(column, inverse)
        x_ref[here, :] = row
        x_ref[here, here] = inverse


def invert(s):
    return pl.pallas_call(
        invert_kernel,
        out_shape=jax.ShapeDtypeStruct((512, 512), F),
        in_specs=[VMEM],
        out_specs=VMEM,
        compiler_params=pltpu.CompilerParams(vmem_limit_bytes=LIMIT),
        name="invert",
    )(s)


def update_kernel(h_hbm, w_hbm, p_ref, x_ref, pan_ref, y_ref, wt_ref, ho_hbm, wo_hbm, hv, wv, sem, osem):
    col = lax.axis_index("col")
    h_copies, w_copies = [], []
    for a in range(3):
        for b in range(3):
            copy = pltpu.make_async_copy(
                w_hbm.at[pl.ds(256 * a, 256), b, 0, :], wv.at[pl.ds(256 * a, 256), pl.ds(256 * b, 256)], sem.at[18 + 3 * a + b]
            )
            copy.start()
            w_copies.append(copy)
    for a in range(6):
        for b in range(3):
            copy = pltpu.make_async_copy(
                h_hbm.at[a, 0, :, b, 0, :], hv.at[pl.ds(256 * a, 256), pl.ds(256 * b, 256)], sem.at[3 * a + b]
            )
            copy.start()
            h_copies.append(copy)
    mixed = split2(dot3(split2(x_ref[...]), split2(pan_ref[...]), NN))
    cols = local_place(p_ref, 16, col)
    lane = lax.broadcasted_iota(jnp.int32, cols.shape, 1)
    hit = [jnp.max((cols == lane + 128 * q).astype(F), axis=0, keepdims=True) for q in range(6)]
    pruned_here = jnp.concatenate(hit, axis=1) > 0.5
    outs = []
    for a in range(3):
        for copy in w_copies[3 * a : 3 * a + 3]:
            copy.wait()
        rows = slice(256 * a, 256 * a + 256)
        wv[rows, :] = jnp.where(pruned_here, 0.0, wv[rows, :] - dot3(split2(wt_ref[:, rows]), mixed, TN))
        for b in range(3):
            copy = pltpu.make_async_copy(
                wv.at[pl.ds(256 * a, 256), pl.ds(256 * b, 256)], wo_hbm.at[pl.ds(256 * a, 256), b, 0, :], osem.at[18 + 3 * a + b]
            )
            copy.start()
            outs.append(copy)
    for a in range(6):
        for copy in h_copies[3 * a : 3 * a + 3]:
            copy.wait()
        rows = slice(256 * a, 256 * a + 256)
        left = y_ref[1 - a % 2, :, 256 * (a // 2) : 256 * (a // 2) + 256]
        hv[rows, :] = hv[rows, :] - dot3(split2(left), mixed, TN)
        for b in range(3):
            copy = pltpu.make_async_copy(
                hv.at[pl.ds(256 * a, 256), pl.ds(256 * b, 256)], ho_hbm.at[a, 0, :, b, 0, :], osem.at[3 * a + b]
            )
            copy.start()
            outs.append(copy)
    for copy in outs:
        copy.wait()


def update(hinverse, pruned, weights, x, pan, y, wt):
    return pl.pallas_call(
        update_kernel,
        out_shape=[jax.ShapeDtypeStruct(hinverse.shape, F), jax.ShapeDtypeStruct(weights.shape, F)],
        in_specs=[ANY, ANY, VMEM, VMEM, VMEM, VMEM, VMEM],
        out_specs=[ANY, ANY],
        scratch_shapes=[
            pltpu.VMEM((1536, 768), F),
            pltpu.VMEM((768, 768), F),
            pltpu.SemaphoreType.DMA((27,)),
            pltpu.SemaphoreType.DMA((27,)),
        ],
        compiler_params=pltpu.CompilerParams(vmem_limit_bytes=LIMIT),
        name="update",
    )(hinverse, weights, pruned, x, pan, y, wt)


def per_device(hinverse, pruned, weights):
    t, wt = gather(hinverse, pruned, weights)
    s, pan, y, w = exchange(t, wt, pruned)
    x = invert(s.reshape(2, 512, 256))
    return update(hinverse, pruned, weights, x, pan.reshape(512, 768), y.reshape(2, 512, 768), w.reshape(512, 768))


def solution(mesh):
    placed = (P(None, "row", None, None, "col", None), P(), P("row", None, "col", None))
    return jax.shard_map(
        per_device,
        mesh=mesh,
        in_specs=placed,
        out_specs=(P(None, "row", None, None, "col", None), P("row", None, "col", None)),
        check_vma=False,
    )
```

```python
import functools

import jax
import jax.numpy as jnp
from jax import lax
from jax.experimental import pallas as pl
from jax.experimental.pallas import tpu as pltpu
from jax.sharding import PartitionSpec as P

F = jnp.float32
B = jnp.bfloat16
MESH = pl.DeviceIdType.MESH
HIGHEST = lax.Precision.HIGHEST
NN = ((1,), (0,))
NT = ((1,), (1,))
TN = ((0,), (0,))
ANY = pl.BlockSpec(memory_space=pl.ANY)
VMEM = pl.BlockSpec(memory_space=pltpu.VMEM)
LIMIT = 56 * 2**20


def split3(x):
    hi = x.astype(B)
    rest = x - hi.astype(F)
    mid = rest.astype(B)
    return hi, mid, (rest - mid.astype(F)).astype(B)


def split2(x):
    hi = x.astype(B)
    return hi, (x - hi.astype(F)).astype(B)


def dot(a, b, dims):
    return lax.dot_general(a, b, (dims, ((), ())), preferred_element_type=F)


def dot3(a, b, dims):
    (ah, al), (bh, bl) = a, b
    return dot(al, bh, dims) + dot(ah, bl, dims) + dot(ah, bh, dims)


def local_place(p_ref, parts, index):
    p = jnp.concatenate([p_ref[0:1, :], p_ref[1:2, :]], axis=1)
    p = jnp.broadcast_to(p, (128, p.shape[1])).T
    tile = p >> 8
    return jnp.where(tile % parts == index, (tile // parts) * 256 + (p & 255), -1)


def onehot(place, start, width):
    lane = lax.broadcasted_iota(jnp.int32, place.shape, 1)
    blocks = [(place == lane + (start + 128 * q)).astype(F).astype(B) for q in range(width // 128)]
    return jnp.concatenate(blocks, axis=1)


class Links:
    def __init__(self, send, recv):
        self.send, self.recv, self.count, self.started = send, recv, 0, []

    def copy(self, src, dst, device):
        n = self.count
        self.count += 1
        made = pltpu.make_async_remote_copy(
            src_ref=src, dst_ref=dst, send_sem=self.send.at[n], recv_sem=self.recv.at[n], device_id=device, device_id_type=MESH
        )
        made.start()
        self.started.append(made)
        return made

    def drain(self):
        for made in self.started:
            made.wait_send()


class RingSum:
    def __init__(self, links, i, up, down, full, half, boxes):
        self.links, self.i, self.up, self.down = links, i, up, down
        self.full, self.half, self.boxes = full, half, boxes

    def far(self):
        left, right, _, _ = self.boxes
        j = (self.i + 2) % 4
        self.a = self.links.copy(self.half(j, 0), left, self.up)
        self.b = self.links.copy(self.half(j, 1), right, self.down)

    def near(self):
        left, right, left2, right2 = self.boxes
        up, down = (self.i + 1) % 4, (self.i + 3) % 4
        self.a.wait_recv()
        part = self.half(up, 0)
        part[...] = part[...] + left[...]
        self.a = self.links.copy(self.full(up), left2, self.up)
        self.b.wait_recv()
        part = self.half(down, 1)
        part[...] = part[...] + right[...]
        self.b = self.links.copy(self.full(down), right2, self.down)

    def finish(self):
        _, _, left2, right2 = self.boxes
        self.a.wait_recv()
        self.b.wait_recv()
        return self.full(self.i)[...] + left2[...] + right2[...]


class RingGather:
    def __init__(self, links, i, up, down, full, half):
        self.links, self.i, self.up, self.down = links, i, up, down
        self.full, self.half = full, half

    def own(self):
        mine = self.full(self.i)
        self.a = self.links.copy(mine, mine, self.up)
        self.b = self.links.copy(mine, mine, self.down)

    def forward(self):
        self.a.wait_recv()
        part = self.half((self.i + 3) % 4, 0)
        self.a = self.links.copy(part, part, self.up)
        self.b.wait_recv()
        part = self.half((self.i + 1) % 4, 1)
        self.b = self.links.copy(part, part, self.down)

    def finish(self):
        self.a.wait_recv()
        self.b.wait_recv()


def sweep8(groups, m):
    n = 8 * len(groups)
    row = groups[m]
    sub = lax.broadcasted_iota(jnp.int32, (8, n), 0)
    lane = lax.broadcasted_iota(jnp.int32, (8, n), 1)
    c = [jnp.broadcast_to(row[:, 8 * m + j : 8 * m + j + 1], (8, n)) for j in range(8)]
    for k in range(8):
        pivot = 1.0 / jnp.broadcast_to(c[k][k : k + 1, :], (8, n))
        at_k = sub == k
        ck = c[k]
        for j in range(8):
            if j != k:
                t = jnp.broadcast_to(c[j][k : k + 1, :], (8, n)) * pivot
                c[j] = jnp.where(at_k, t, c[j] - ck * t)
        c[k] = jnp.where(at_k, pivot, -(ck * pivot))
    inside = (lane >= 8 * m) & (lane < 8 * m + 8)
    row = jnp.where(inside, jnp.where(lane - 8 * m == sub, 1.0, 0.0), row)
    new = c[0] * jnp.broadcast_to(row[0:1, :], (8, n))
    for j in range(1, 8):
        new = new + c[j] * jnp.broadcast_to(row[j : j + 1, :], (8, n))
    spread = [jnp.broadcast_to(new[j : j + 1, :], (8, n)) for j in range(8)]
    out = []
    for i, group in enumerate(groups):
        if i == m:
            out.append(new)
            continue
        left = jnp.where(inside, 0.0, group)
        for j in range(8):
            left = left - jnp.broadcast_to(group[:, 8 * m + j : 8 * m + j + 1], (8, n)) * spread[j]
        out.append(left)
    return out


def invert128(block):
    groups = [block[8 * i : 8 * i + 8, :] for i in range(16)]
    for m in range(16):
        groups = sweep8(groups, m)
    return jnp.concatenate(groups, axis=0)


def fdot(a, b):
    return jnp.dot(a, b, precision=HIGHEST, preferred_element_type=F)


def invert_block(x, k):
    here = slice(128 * k, 128 * k + 128)
    inverse = invert128(x[here, here])
    row = fdot(inverse, x[here, :])
    column = x[:, here]
    x[...] = x[...] - fdot(column, row)
    x[:, here] = -fdot(column, inverse)
    x[here, :] = row
    x[here, here] = inverse


def main_kernel(h_hbm, w_hbm, p_ref, m_hbm, y_hbm, wo_hbm,
                hv, wv, parts, place, t, ra, xbox1, xbox2, wt, wc, wboxf, wboxn, wbox2f, wbox2n,
                sm, srx, s, pan, ya, y, w, xs, mv, send, recv, isem, osem):
    row = lax.axis_index("row")
    col = lax.axis_index("col")
    x, k = row // 2, row % 2
    z, yy = col // 4, col % 4

    def dev(r, c):
        return {"row": r, "col": c}

    sibling = dev(2 * x + 1 - k, col)
    x_up, x_down = dev((row + 2) % 8, col), dev((row + 6) % 8, col)
    y_up, y_down = dev(row, 4 * z + (yy + 1) % 4), dev(row, 4 * z + (yy + 3) % 4)
    z_up, z_down = dev(row, (col + 4) % 16), dev(row, (col + 12) % 16)
    target = dev(col % 8, 4 * (2 * (1 - col // 8) + k) + x)
    source = dev(2 * yy + z % 2, row + 8 * (1 - z // 2))
    peers = [dev(row, (col + d) % 16) for d in range(1, 16)]

    h_copies, w_copies = [], []
    for a in range(6):
        for b in range(3):
            copy = pltpu.make_async_copy(
                h_hbm.at[a, 0, :, b, 0, :], hv.at[pl.ds(256 * a, 256), pl.ds(256 * b, 256)], isem.at[3 * a + b]
            )
            copy.start()
            h_copies.append(copy)
    for b in range(3):
        copy = pltpu.make_async_copy(w_hbm.at[:, b, 0, :], wv.at[:, pl.ds(256 * b, 256)], isem.at[18 + b])
        copy.start()
        w_copies.append(copy)

    barrier = pltpu.get_barrier_semaphore()
    greet = [sibling, x_up, x_down, target, source] + peers
    for device in greet:
        pl.semaphore_signal(barrier, inc=1, device_id=device, device_id_type=MESH)

    place[...] = local_place(p_ref, 8, row).reshape(4, 2, 64, 128)
    cols = local_place(p_ref, 16, col)

    def masked_rows(half, first):
        where = place[:, half].reshape(256, 128)
        for a in range(6):
            here = slice(256 * a, 256 * a + 256)
            if first:
                for copy in h_copies[3 * a : 3 * a + 3]:
                    copy.wait()
                hi, mid, lo = split3(hv[here, :])
                parts[0, here, :] = hi
                parts[1, here, :] = mid
                parts[2, here, :] = lo
            hot = onehot(where, 256 * a, 256)
            part = dot(hot, parts[2, here, :], NN) + dot(hot, parts[1, here, :], NN) + dot(hot, parts[0, here, :], NN)
            part = part.reshape(4, 64, 768)
            t[:, half] = part if a == 0 else t[:, half] + part

    masked_rows(1 - k, True)
    pl.semaphore_wait(barrier, len(greet))
    links = Links(send, recv)
    order = [(x + 2) % 4, (x + 1) % 4, (x + 3) % 4, x]
    halves = [links.copy(t.at[j, 1 - k], ra.at[j], sibling) for j in order]
    masked_rows(k, False)
    sum_x = RingSum(links, x, x_up, x_down, lambda j: ra.at[j], lambda j, h: ra.at[j, pl.ds(32 * h, 32)],
                    (xbox1.at[0], xbox1.at[1], xbox2.at[0], xbox2.at[1]))
    for n, j in enumerate(order):
        halves[n].wait_recv()
        ra[j] = ra[j] + t[j, k]
        if n == 0:
            sum_x.far()

    for b in range(3):
        w_copies[b].wait()
        hot = onehot(cols, 256 * b, 256)
        hi, mid, lo = split3(wv[:, 256 * b : 256 * b + 256])
        part = dot(lo, hot, NT) + dot(mid, hot, NT) + dot(hi, hot, NT)
        part = part.reshape(4, 4, 48, 512)
        wt[...] = part if b == 0 else wt[...] + part

    lanes = [pl.ds(0, 256), pl.ds(256, 256)]
    sum_z0 = RingSum(links, z, z_up, z_down, lambda j: wt.at[j, :, :, lanes[0]],
                     lambda j, h: wt.at[j, pl.ds(2 * h, 2), :, lanes[0]],
                     (wboxf.at[0], wboxf.at[1], wboxn.at[0], wboxn.at[1]))
    sum_y1 = RingSum(links, yy, y_up, y_down, lambda j: wt.at[:, j, :, lanes[1]],
                     lambda j, h: wt.at[pl.ds(2 * h, 2), j, :, lanes[1]],
                     (wboxf.at[2], wboxf.at[3], wboxn.at[2], wboxn.at[3]))
    sum_y0 = RingSum(links, yy, y_up, y_down, lambda j: wc.at[0, j], lambda j, h: wc.at[0, j, pl.ds(24 * h, 24)],
                     (wbox2f.at[0], wbox2f.at[1], wbox2n.at[0], wbox2n.at[1]))
    sum_z1 = RingSum(links, z, z_up, z_down, lambda j: wc.at[1, j], lambda j, h: wc.at[1, j, pl.ds(24 * h, 24)],
                     (wbox2f.at[2], wbox2f.at[3], wbox2n.at[2], wbox2n.at[3]))
    sum_z0.far()
    sum_y1.far()
    sum_x.near()
    sum_z0.near()
    sum_y1.near()

    pan[x, k] = sum_x.finish()
    mine = pan.at[x, k]
    paired = links.copy(mine, mine, sibling)
    total = jnp.zeros((64, 512), F)
    for b in range(3):
        hot = onehot(cols, 256 * b, 256)
        hi, mid, lo = split3(pan[x, k, :, 256 * b : 256 * b + 256])
        total = total + (dot(lo, hot, NT) + dot(mid, hot, NT) + dot(hi, hot, NT))
    sm[0] = total[:, :256].reshape(8, 8, 256)
    sm[1] = total[:, 256:].reshape(8, 8, 256)
    summed = []
    for d in range(1, 16):
        q = (col + d) % 16
        summed.append(links.copy(sm.at[q % 2, q // 2], srx.at[d - 1], peers[d - 1]))

    paired.wait_recv()
    start = pl.multiple_of(384 * k, 128)
    ya[...] = pan[x, :, :, pl.ds(start, 384)].reshape(128, 384).T

    def lane_block(j):
        return pl.ds(pl.multiple_of(128 * j, 128), 128)

    moved = links.copy(ya, y.at[2 * (1 - col // 8) + k, :, lane_block(x)], target)

    wc[0] = sum_z0.finish()
    wc[1] = sum_y1.finish()
    sum_y0.far()
    sum_z1.far()

    piece = sm[col % 2, col // 2]
    for d in range(1, 16):
        summed[d - 1].wait_recv()
        piece = piece + srx[d - 1]
    own_s = s.at[col % 2, x, k, pl.ds(pl.multiple_of(8 * (col // 2), 8), 8)]
    own_s[...] = piece
    spread = [links.copy(own_s, own_s, peers[d - 1]) for d in range(1, 16)]

    sum_y0.near()
    sum_z1.near()

    moved.wait_recv()
    upper, lower = pl.ds(0, 192), pl.ds(192, 192)
    y_y0 = RingGather(links, yy, y_up, y_down, lambda j: y.at[z, upper, lane_block(j)],
                      lambda j, h: y.at[z, pl.ds(96 * h, 96), lane_block(j)])
    y_z1 = RingGather(links, z, z_up, z_down, lambda j: y.at[j, lower, lane_block(yy)],
                      lambda j, h: y.at[j, pl.ds(192 + 96 * h, 96), lane_block(yy)])
    y_z0 = RingGather(links, z, z_up, z_down, lambda j: y.at[j, upper],
                      lambda j, h: y.at[j, pl.ds(96 * h, 96)])
    y_y1 = RingGather(links, yy, y_up, y_down, lambda j: y.at[:, lower, lane_block(j)],
                      lambda j, h: y.at[pl.ds(2 * h, 2), lower, lane_block(j)])
    y_y0.own()
    y_z1.own()

    for copy in spread:
        copy.wait_recv()
    s_x = RingGather(links, x, x_up, x_down, lambda j: s.at[:, j, k], lambda j, h: s.at[h, j, k])
    s_x.own()

    w[z, yy, :, 0:256] = sum_y0.finish()
    w[z, yy, :, 256:512] = sum_z1.finish()
    w_y0 = RingGather(links, yy, y_up, y_down, lambda j: w.at[z, j, :, lanes[0]],
                      lambda j, h: w.at[z, j, pl.ds(24 * h, 24), lanes[0]])
    w_z1 = RingGather(links, z, z_up, z_down, lambda j: w.at[j, yy, :, lanes[1]],
                      lambda j, h: w.at[j, yy, pl.ds(24 * h, 24), lanes[1]])
    w_z0 = RingGather(links, z, z_up, z_down, lambda j: w.at[j, :, :, lanes[0]],
                      lambda j, h: w.at[j, pl.ds(2 * h, 2), :, lanes[0]])
    w_y1 = RingGather(links, yy, y_up, y_down, lambda j: w.at[:, j, :, lanes[1]],
                      lambda j, h: w.at[pl.ds(2 * h, 2), j, :, lanes[1]])
    w_y0.own()
    w_z1.own()

    s_x.forward()
    pan_x = RingGather(links, x, x_up, x_down, lambda j: pan.at[j, k], lambda j, h: pan.at[j, k, pl.ds(32 * h, 32)])
    pan_x.own()
    y_y0.forward()
    y_z1.forward()
    w_y0.forward()
    w_z1.forward()
    s_x.finish()
    mine_s = s.at[:, :, k]
    swap_s = links.copy(mine_s, mine_s, sibling)
    y_y0.finish()
    y_z0.own()
    y_z1.finish()
    y_y1.own()
    w_y0.finish()
    w_z0.own()
    w_z1.finish()
    w_y1.own()

    swap_s.wait_recv()
    xs[:, 0:256] = s[0].reshape(512, 256)
    xs[:, 256:512] = s[1].reshape(512, 256)
    invert_block(xs, 0)
    pan_x.forward()
    invert_block(xs, 1)
    y_z0.forward()
    y_y1.forward()
    w_z0.forward()
    w_y1.forward()
    pan_x.finish()
    swaps = []
    for n in range(1, 4):
        part = pan.at[(x + n) % 4, k]
        swaps.append(links.copy(part, part, sibling))
    invert_block(xs, 2)
    invert_block(xs, 3)
    y_z0.finish()
    y_y1.finish()
    outs = [pltpu.make_async_copy(y, y_hbm, osem.at[0])]
    outs[0].start()
    for copy in swaps:
        copy.wait_recv()
    a = split2(xs[...])
    b = split2(pan[...].reshape(512, 768))
    hi, lo = split2(dot3(a, b, NN))
    mv[0] = hi
    mv[1] = lo
    outs.append(pltpu.make_async_copy(mv, m_hbm, osem.at[1]))
    outs[1].start()
    w_z0.finish()
    w_y1.finish()
    outs.append(pltpu.make_async_copy(w, wo_hbm, osem.at[2]))
    outs[2].start()
    for copy in outs:
        copy.wait()
    links.drain()


COPIES = 100


def solve(hinverse, pruned, weights):
    return pl.pallas_call(
        main_kernel,
        out_shape=[
            jax.ShapeDtypeStruct((2, 512, 768), B),
            jax.ShapeDtypeStruct((4, 384, 512), F),
            jax.ShapeDtypeStruct((4, 4, 48, 512), F),
        ],
        in_specs=[ANY, ANY, VMEM],
        out_specs=[ANY] * 3,
        scratch_shapes=[
            pltpu.VMEM((1536, 768), F),
            pltpu.VMEM((768, 768), F),
            pltpu.VMEM((3, 1536, 768), B),
            pltpu.VMEM((4, 2, 64, 128), jnp.int32),
            pltpu.VMEM((4, 2, 64, 768), F),
            pltpu.VMEM((4, 64, 768), F),
            pltpu.VMEM((2, 32, 768), F),
            pltpu.VMEM((2, 64, 768), F),
            pltpu.VMEM((4, 4, 48, 512), F),
            pltpu.VMEM((2, 4, 48, 256), F),
            pltpu.VMEM((4, 2, 48, 256), F),
            pltpu.VMEM((4, 4, 48, 256), F),
            pltpu.VMEM((4, 24, 256), F),
            pltpu.VMEM((4, 48, 256), F),
            pltpu.VMEM((2, 8, 8, 256), F),
            pltpu.VMEM((15, 8, 256), F),
            pltpu.VMEM((2, 4, 2, 64, 256), F),
            pltpu.VMEM((4, 2, 64, 768), F),
            pltpu.VMEM((384, 128), F),
            pltpu.VMEM((4, 384, 512), F),
            pltpu.VMEM((4, 4, 48, 512), F),
            pltpu.VMEM((512, 512), F),
            pltpu.VMEM((2, 512, 768), B),
            pltpu.SemaphoreType.DMA((COPIES,)),
            pltpu.SemaphoreType.DMA((COPIES,)),
            pltpu.SemaphoreType.DMA((21,)),
            pltpu.SemaphoreType.DMA((3,)),
        ],
        compiler_params=pltpu.CompilerParams(vmem_limit_bytes=LIMIT, collective_id=0, has_side_effects=True),
        name="solve",
    )(hinverse, weights, pruned)


def update_kernel(h_hbm, w_hbm, p_ref, m_hbm, y_hbm, wt_hbm, ho_hbm, wo_hbm, hv, wv, mm, yv, wt, sem, osem):
    col = lax.axis_index("col")
    count = [0]

    def fetch(src, dst):
        copy = pltpu.make_async_copy(src, dst, sem.at[count[0]])
        count[0] += 1
        copy.start()
        return copy

    def h_parts(block):
        hi, half = 1 - block // 2, block % 2
        starts = [384 * half + 128 * u for u in range(3)]
        return [(2 * (j // 256) + hi, j % 256) for j in starts]

    m_copies = [fetch(m_hbm.at[0], mm.at[pl.ds(0, 512)]), fetch(m_hbm.at[1], mm.at[pl.ds(512, 512)]),
                fetch(m_hbm.at[0], mm.at[pl.ds(1024, 512)])]
    loads = []
    for g in range(2):
        rows = pl.ds(384 * g, 384)
        loads.append([fetch(wt_hbm.at[rows], wt.at[rows])]
                     + [fetch(w_hbm.at[rows, b, 0, :], wv.at[rows, pl.ds(256 * b, 256)]) for b in range(3)])
    for block in range(4):
        copies = [fetch(y_hbm.at[block], yv.at[block])]
        for u, (a, j) in enumerate(h_parts(block)):
            rows = pl.ds(384 * block + 128 * u, 128)
            copies += [fetch(h_hbm.at[a, 0, pl.ds(j, 128), b, 0, :], hv.at[rows, pl.ds(256 * b, 256)]) for b in range(3)]
        loads.append(copies)
    cols = local_place(p_ref, 16, col)
    lane = lax.broadcasted_iota(jnp.int32, cols.shape, 1)
    hit = [jnp.max((cols == lane + 128 * q).astype(F), axis=0, keepdims=True) for q in range(6)]
    pruned_here = jnp.concatenate(hit, axis=1) > 0.5
    outs = []

    def put(src, dst):
        copy = pltpu.make_async_copy(src, dst, osem.at[len(outs)])
        copy.start()
        outs.append(copy)

    def product(left):
        hi, lo = split2(left)
        return dot(jnp.concatenate([hi, hi, lo], axis=1), mm[...], NN)

    for copy in m_copies:
        copy.wait()
    for g in range(2):
        for copy in loads[g]:
            copy.wait()
        rows = slice(384 * g, 384 * g + 384)
        wv[rows, :] = jnp.where(pruned_here, 0.0, wv[rows, :] - product(wt[rows, :]))
        for b in range(3):
            put(wv.at[pl.ds(384 * g, 384), pl.ds(256 * b, 256)], wo_hbm.at[pl.ds(384 * g, 384), b, 0, :])
    for block in range(4):
        for copy in loads[2 + block]:
            copy.wait()
        rows = slice(384 * block, 384 * block + 384)
        hv[rows, :] = hv[rows, :] - product(yv[block])
        for u, (a, j) in enumerate(h_parts(block)):
            for b in range(3):
                put(hv.at[pl.ds(384 * block + 128 * u, 128), pl.ds(256 * b, 256)], ho_hbm.at[a, 0, pl.ds(j, 128), b, 0, :])
    for copy in outs:
        copy.wait()


def update(hinverse, pruned, weights, m, y, wt):
    return pl.pallas_call(
        update_kernel,
        out_shape=[jax.ShapeDtypeStruct(hinverse.shape, F), jax.ShapeDtypeStruct(weights.shape, F)],
        in_specs=[ANY, ANY, VMEM, ANY, ANY, ANY],
        out_specs=[ANY, ANY],
        scratch_shapes=[
            pltpu.VMEM((1536, 768), F),
            pltpu.VMEM((768, 768), F),
            pltpu.VMEM((1536, 768), B),
            pltpu.VMEM((4, 384, 512), F),
            pltpu.VMEM((768, 512), F),
            pltpu.SemaphoreType.DMA((51,)),
            pltpu.SemaphoreType.DMA((42,)),
        ],
        compiler_params=pltpu.CompilerParams(vmem_limit_bytes=LIMIT),
        name="update",
    )(hinverse, weights, pruned, m, y, wt)


def per_device(hinverse, pruned, weights):
    m, y, w = solve(hinverse, pruned, weights)
    return update(hinverse, pruned, weights, m, y, w.reshape(768, 512))


def solution(mesh):
    placed = (P(None, "row", None, None, "col", None), P(), P("row", None, "col", None))
    return jax.shard_map(
        per_device,
        mesh=mesh,
        in_specs=placed,
        out_specs=(P(None, "row", None, None, "col", None), P("row", None, "col", None)),
        check_vma=False,
    )
```

```python
import jax
import jax.numpy as jnp
from jax import lax
from jax.experimental import pallas as pl
from jax.experimental.pallas import tpu as pltpu
from jax.sharding import PartitionSpec as P

F = jnp.float32
B = jnp.bfloat16
MESH = pl.DeviceIdType.MESH
HIGHEST = lax.Precision.HIGHEST
NN = ((1,), (0,))
NT = ((1,), (1,))
TN = ((0,), (0,))
ANY = pl.BlockSpec(memory_space=pl.ANY)
VMEM = pl.BlockSpec(memory_space=pltpu.VMEM)
MIB = 2**20


def split3(x):
    hi = x.astype(B)
    rest = x - hi.astype(F)
    mid = rest.astype(B)
    return hi, mid, (rest - mid.astype(F)).astype(B)


def split2(x):
    hi = x.astype(B)
    return hi, (x - hi.astype(F)).astype(B)


def dot(a, b, dims):
    return lax.dot_general(a, b, (dims, ((), ())), preferred_element_type=F)


def dot3(a, b, dims):
    (ah, al), (bh, bl) = a, b
    return dot(al, bh, dims) + dot(ah, bl, dims) + dot(ah, bh, dims)


def local_place(p_ref, parts, index):
    p = jnp.concatenate([p_ref[0:1, :], p_ref[1:2, :]], axis=1)
    p = jnp.broadcast_to(p, (128, p.shape[1])).T
    tile = p >> 8
    return jnp.where(tile % parts == index, (tile // parts) * 256 + (p & 255), -1)


def onehot(place, start, width):
    lane = lax.broadcasted_iota(jnp.int32, place.shape, 1)
    blocks = [(place == lane + (start + 128 * q)).astype(F).astype(B) for q in range(width // 128)]
    return jnp.concatenate(blocks, axis=1)


class Links:
    def __init__(self, send, recv):
        self.send, self.recv, self.count, self.started = send, recv, 0, []

    def copy(self, src, dst, device):
        n = self.count
        self.count += 1
        made = pltpu.make_async_remote_copy(
            src_ref=src, dst_ref=dst, send_sem=self.send.at[n], recv_sem=self.recv.at[n], device_id=device, device_id_type=MESH
        )
        made.start()
        self.started.append(made)
        return made

    def drain(self):
        for made in self.started:
            made.wait_send()


def halves_of(ref):
    n = ref.shape[0] // 2
    return ref.at[pl.ds(0, n)], ref.at[pl.ds(n, n)]


class RingSum:
    def __init__(self, links, i, up, down, full, boxes):
        self.links, self.i, self.up, self.down, self.full, self.boxes = links, i, up, down, full, boxes

    def start(self):
        left, right, left2, right2 = self.boxes
        far0, far1 = halves_of(self.full((self.i + 2) % 4))
        self.a = self.links.copy(far0, left, self.up)
        self.b = self.links.copy(far1, right, self.down)
        self.c = self.links.copy(halves_of(self.full((self.i + 1) % 4))[1], halves_of(left2)[1], self.up)
        self.d = self.links.copy(halves_of(self.full((self.i + 3) % 4))[0], halves_of(right2)[0], self.down)

    def near(self):
        left, right, left2, right2 = self.boxes
        self.a.wait_recv()
        part = halves_of(self.full((self.i + 1) % 4))[0]
        part[...] = part[...] + left[...]
        self.a = self.links.copy(part, halves_of(left2)[0], self.up)
        self.b.wait_recv()
        part = halves_of(self.full((self.i + 3) % 4))[1]
        part[...] = part[...] + right[...]
        self.b = self.links.copy(part, halves_of(right2)[1], self.down)

    def finish(self):
        _, _, left2, right2 = self.boxes
        for copy in (self.a, self.b, self.c, self.d):
            copy.wait_recv()
        return self.full(self.i)[...] + left2[...] + right2[...]


class RingGather:
    def __init__(self, links, i, up, down, full):
        self.links, self.i, self.up, self.down, self.full = links, i, up, down, full

    def own(self):
        first, second = halves_of(self.full(self.i))
        self.a = self.links.copy(first, first, self.up)
        self.b = self.links.copy(second, second, self.down)
        self.c = self.links.copy(second, second, self.up)
        self.d = self.links.copy(first, first, self.down)

    def forward(self):
        self.a.wait_recv()
        part = halves_of(self.full((self.i + 3) % 4))[0]
        self.a = self.links.copy(part, part, self.up)
        self.b.wait_recv()
        part = halves_of(self.full((self.i + 1) % 4))[1]
        self.b = self.links.copy(part, part, self.down)

    def finish(self):
        for copy in (self.a, self.b, self.c, self.d):
            copy.wait_recv()


def sweep8(groups, m):
    n = 8 * len(groups)
    row = groups[m]
    sub = lax.broadcasted_iota(jnp.int32, (8, n), 0)
    lane = lax.broadcasted_iota(jnp.int32, (8, n), 1)
    c = [jnp.broadcast_to(row[:, 8 * m + j : 8 * m + j + 1], (8, n)) for j in range(8)]
    for k in range(8):
        pivot = 1.0 / jnp.broadcast_to(c[k][k : k + 1, :], (8, n))
        at_k = sub == k
        ck = c[k]
        for j in range(8):
            if j != k:
                t = jnp.broadcast_to(c[j][k : k + 1, :], (8, n)) * pivot
                c[j] = jnp.where(at_k, t, c[j] - ck * t)
        c[k] = jnp.where(at_k, pivot, -(ck * pivot))
    inside = (lane >= 8 * m) & (lane < 8 * m + 8)
    row = jnp.where(inside, jnp.where(lane - 8 * m == sub, 1.0, 0.0), row)
    new = c[0] * jnp.broadcast_to(row[0:1, :], (8, n))
    for j in range(1, 8):
        new = new + c[j] * jnp.broadcast_to(row[j : j + 1, :], (8, n))
    spread = [jnp.broadcast_to(new[j : j + 1, :], (8, n)) for j in range(8)]
    out = []
    for i, group in enumerate(groups):
        if i == m:
            out.append(new)
            continue
        left = jnp.where(inside, 0.0, group)
        for j in range(8):
            left = left - jnp.broadcast_to(group[:, 8 * m + j : 8 * m + j + 1], (8, n)) * spread[j]
        out.append(left)
    return out


def fdot(a, b):
    return jnp.dot(a, b, precision=HIGHEST, preferred_element_type=F)


def invert128(block, between):
    groups = [block[8 * i : 8 * i + 8, :] for i in range(16)]
    for m in range(16):
        groups = sweep8(groups, m)
        if m == 7:
            between()
    return jnp.concatenate(groups, axis=0)


def invert_block(x, k, between):
    here = slice(128 * k, 128 * k + 128)
    inverse = invert128(x[here, here], between)
    row = fdot(inverse, x[here, :])
    column = x[:, here]
    x[...] = x[...] - fdot(column, row)
    x[:, here] = -fdot(column, inverse)
    x[here, :] = row
    x[here, here] = inverse


def gather_kernel(h_hbm, w_hbm, p_smem, p_ref, t_ref, wt_ref, sc_ref, hv, wv, sem):
    row = lax.axis_index("row")
    col = lax.axis_index("col")
    w_copies, h_copies = [], []
    for b in range(3):
        copy = pltpu.make_async_copy(w_hbm.at[:, b, 0, :], wv.at[:, pl.ds(256 * b, 256)], sem.at[18 + b])
        copy.start()
        w_copies.append(copy)
    for a in range(6):
        for b in range(3):
            copy = pltpu.make_async_copy(
                h_hbm.at[a, 0, :, b, 0, :], hv.at[pl.ds(256 * a, 256), pl.ds(256 * b, 256)], sem.at[3 * a + b]
            )
            copy.start()
            h_copies.append(copy)
    cols = local_place(p_ref, 16, col)
    hot = [onehot(cols, 256 * b, 256) for b in range(3)]
    for b in range(3):
        w_copies[b].wait()
        hi, mid, lo = split3(wv[:, 256 * b : 256 * b + 256])
        part = dot(lo, hot[b], NT) + dot(mid, hot[b], NT) + dot(hi, hot[b], NT)
        wt_ref[...] = part if b == 0 else wt_ref[...] + part
    for copy in h_copies:
        copy.wait()

    def eight(g, _):
        for j in range(8):
            i = 8 * g + j
            p = p_smem[i // 256, i % 256]
            tile = p // 256
            mine = tile % 8 == row
            at = jnp.where(mine, (tile // 8) * 256 + p % 256, 0)
            t_ref[pl.ds(i, 1), :] = jnp.where(mine, hv[pl.ds(at, 1), :], 0.0)
        return 0

    lax.fori_loop(0, 64, eight, 0)
    total = None
    for b in range(3):
        hi, mid, lo = split3(t_ref[:, 256 * b : 256 * b + 256])
        part = dot(lo, hot[b], NT) + dot(mid, hot[b], NT) + dot(hi, hot[b], NT)
        total = part if b == 0 else total + part
    for v in range(2):
        for j in range(2):
            lanes = slice(256 * v + 128 * j, 256 * v + 128 * j + 128)
            sc_ref[:, v, :, :, j] = total[:, lanes].reshape(4, 2, 8, 8, 128).transpose(1, 0, 2, 3, 4)


def gather(hinverse, pruned, weights):
    return pl.pallas_call(
        gather_kernel,
        out_shape=[
            jax.ShapeDtypeStruct((512, 768), F),
            jax.ShapeDtypeStruct((768, 512), F),
            jax.ShapeDtypeStruct((2, 2, 4, 8, 2, 8, 128), F),
        ],
        in_specs=[ANY, ANY, pl.BlockSpec(memory_space=pltpu.SMEM), VMEM],
        out_specs=[VMEM] * 3,
        scratch_shapes=[
            pltpu.VMEM((1536, 768), F),
            pltpu.VMEM((768, 768), F),
            pltpu.SemaphoreType.DMA((21,)),
        ],
        compiler_params=pltpu.CompilerParams(vmem_limit_bytes=32 * MIB),
        name="gather",
    )(hinverse, weights, pruned, pruned)


def solve_kernel(t, wt, sc, m_hbm, y_hbm, wo_hbm,
                 ra, xbox1, xbox2, wc, wboxf, wboxn, wbox2f, wbox2n,
                 sbox, px, qy, ps, qs, py, qx, sf, pan, ya, y, w, xs, mv, send, recv, osem):
    row = lax.axis_index("row")
    col = lax.axis_index("col")
    x, k = row // 2, row % 2
    z, yy = col // 4, col % 4
    cu, cl = col // 2, col % 2

    def dev(r, c):
        return {"row": r, "col": c}

    sibling = dev(2 * x + 1 - k, col)
    x_peers = [dev((row + 2 * d) % 8, col) for d in range(1, 4)]
    peers = [dev(row, (col + d) % 16) for d in range(1, 16)]
    x_up, x_down = x_peers[0], x_peers[2]
    y_up, y_down = dev(row, 4 * z + (yy + 1) % 4), dev(row, 4 * z + (yy + 3) % 4)
    z_up, z_down = peers[3], peers[11]
    target = dev(col % 8, 4 * (2 * (1 - col // 8) + k) + x)
    source = dev(2 * yy + z % 2, row + 8 * (1 - z // 2))

    barrier = pltpu.get_barrier_semaphore()
    greet = [sibling, target, source] + x_peers + peers
    for device in greet:
        pl.semaphore_signal(barrier, inc=1, device_id=device, device_id_type=MESH)
    pl.semaphore_wait(barrier, len(greet))
    links = Links(send, recv)

    first = [links.copy(sc.at[1 - k, v], sbox.at[v], sibling) for v in range(2)]
    order = [(x + 2) % 4, (x + 1) % 4, (x + 3) % 4, x]
    rows_in = [links.copy(t.at[j, 1 - k], ra.at[j], sibling) for j in order]

    lanes = [pl.ds(0, 256), pl.ds(256, 256)]
    sum_z0 = RingSum(links, z, z_up, z_down, lambda j: wt.at[j, :, :, lanes[0]],
                     (wboxf.at[0], wboxf.at[1], wboxn.at[0], wboxn.at[1]))
    sum_y1 = RingSum(links, yy, y_up, y_down, lambda j: wt.at[:, j, :, lanes[1]],
                     (wboxf.at[2], wboxf.at[3], wboxn.at[2], wboxn.at[3]))
    sum_y0 = RingSum(links, yy, y_up, y_down, lambda j: wc.at[0, j],
                     (wbox2f.at[0], wbox2f.at[1], wbox2n.at[0], wbox2n.at[1]))
    sum_z1 = RingSum(links, z, z_up, z_down, lambda j: wc.at[1, j],
                     (wbox2f.at[2], wbox2f.at[3], wbox2n.at[2], wbox2n.at[3]))
    sum_x = RingSum(links, x, x_up, x_down, lambda j: ra.at[j],
                    (xbox1.at[0], xbox1.at[1], xbox2.at[0], xbox2.at[1]))

    first[0].wait_recv()
    sbox[0] = sbox[0] + sc[k, 0]
    p1 = [links.copy(sbox.at[0, (x + d) % 4], px.at[d - 1], x_peers[d - 1]) for d in range(1, 4)]
    first[1].wait_recv()
    sbox[1] = sbox[1] + sc[k, 1]
    q1 = []
    for d in range(1, 16):
        q = (col + d) % 16
        q1.append(links.copy(sbox.at[1, :, q // 2, q % 2], qy.at[d - 1], peers[d - 1]))
    sum_z0.start()
    sum_y1.start()

    for n, j in enumerate(order):
        rows_in[n].wait_recv()
        ra[j] = ra[j] + t[j, k]
    sum_x.start()

    total = sbox[0, x]
    for d in range(1, 4):
        p1[d - 1].wait_recv()
        total = total + px[d - 1]
    ps[...] = total
    p2 = []
    for d in range(1, 16):
        q = (col + d) % 16
        p2.append(links.copy(ps.at[q // 2, q % 2], py.at[d - 1], peers[d - 1]))
    total = sbox[1, :, cu, cl]
    for d in range(1, 16):
        q1[d - 1].wait_recv()
        total = total + qy[d - 1]
    qs[...] = total
    q2 = [links.copy(qs.at[(x + d) % 4], qx.at[d - 1], x_peers[d - 1]) for d in range(1, 4)]

    sum_x.near()
    sum_z0.near()
    sum_y1.near()

    total = qs[x]
    for d in range(1, 4):
        q2[d - 1].wait_recv()
        total = total + qx[d - 1]
    own_q = sf.at[k, 1, x, cu, cl]
    own_q[...] = total
    q3 = [links.copy(own_q, own_q, x_peers[d - 1]) for d in range(1, 4)]
    total = ps[cu, cl]
    for d in range(1, 16):
        p2[d - 1].wait_recv()
        total = total + py[d - 1]
    own_p = sf.at[k, 0, x, cu, cl]
    own_p[...] = total
    p3 = [links.copy(own_p, own_p, peers[d - 1]) for d in range(1, 16)]

    for copy in q3:
        copy.wait_recv()
    own_q = sf.at[k, 1, :, cu, cl]
    q4 = [links.copy(own_q, own_q, peers[d - 1]) for d in range(1, 16)]
    for copy in p3:
        copy.wait_recv()
    own_p = sf.at[k, 0, x]
    p4 = [links.copy(own_p, own_p, x_peers[d - 1]) for d in range(1, 4)]

    wc[0] = sum_z0.finish()
    wc[1] = sum_y1.finish()
    sum_y0.start()
    sum_z1.start()

    pan[x, k] = sum_x.finish()
    mine = pan.at[x, k]
    paired = links.copy(mine, mine, sibling)
    sum_y0.near()
    sum_z1.near()

    paired.wait_recv()
    start = pl.multiple_of(384 * k, 128)
    ya[...] = pan[x, :, :, pl.ds(start, 384)].reshape(128, 384).T

    def lane_block(j):
        return pl.ds(pl.multiple_of(128 * j, 128), 128)

    moved = links.copy(ya, y.at[2 * (1 - col // 8) + k, :, lane_block(x)], target)

    for copy in q4 + p4:
        copy.wait_recv()
    own_s = sf.at[k]
    swap_s = links.copy(own_s, own_s, sibling)

    w[z, yy, :, 0:256] = sum_y0.finish()
    w[z, yy, :, 256:512] = sum_z1.finish()
    w_y0 = RingGather(links, yy, y_up, y_down, lambda j: w.at[z, j, :, lanes[0]])
    w_z1 = RingGather(links, z, z_up, z_down, lambda j: w.at[j, yy, :, lanes[1]])
    w_z0 = RingGather(links, z, z_up, z_down, lambda j: w.at[j, :, :, lanes[0]])
    w_y1 = RingGather(links, yy, y_up, y_down, lambda j: w.at[:, j, :, lanes[1]])
    upper, lower = pl.ds(0, 192), pl.ds(192, 192)
    y_y0 = RingGather(links, yy, y_up, y_down, lambda j: y.at[z, upper, lane_block(j)])
    y_z1 = RingGather(links, z, z_up, z_down, lambda j: y.at[j, lower, lane_block(yy)])
    y_z0 = RingGather(links, z, z_up, z_down, lambda j: y.at[j, upper])
    y_y1 = RingGather(links, yy, y_up, y_down, lambda j: y.at[:, lower, lane_block(j)])
    pan_x = RingGather(links, x, x_up, x_down, lambda j: pan.at[j, k])
    w_y0.own()
    w_z1.own()

    swap_s.wait_recv()
    for v in range(2):
        for j in range(2):
            xs[:, 256 * v + 128 * j : 256 * v + 128 * j + 128] = sf[:, v, :, :, j].transpose(1, 0, 2, 3, 4).reshape(512, 128)
    pan_x.own()
    w_y0.forward()
    w_z1.forward()

    swaps = []

    def after_0():
        moved.wait_recv()
        y_y0.own()
        y_z1.own()
        w_y0.finish()
        w_z1.finish()

    def after_1():
        y_y0.forward()
        y_z1.forward()
        w_z0.own()
        w_y1.own()
        pan_x.forward()

    def after_2():
        y_y0.finish()
        y_z0.own()
        y_z1.finish()
        y_y1.own()

    def after_3():
        pan_x.finish()
        for n in range(1, 4):
            part = pan.at[(x + n) % 4, k]
            swaps.append(links.copy(part, part, sibling))

    def after_4():
        w_z0.forward()
        w_y1.forward()

    def after_5():
        y_z0.forward()
        y_y1.forward()

    def nothing():
        pass

    invert_block(xs, 0, after_0)
    after_1()
    invert_block(xs, 1, after_2)
    after_3()
    invert_block(xs, 2, after_4)
    after_5()
    invert_block(xs, 3, nothing)
    for copy in swaps:
        copy.wait_recv()
    a = split2(xs[...])
    b = split2(pan[...].reshape(512, 768))
    hi, lo = split2(dot3(a, b, NN))
    mv[0] = hi
    mv[1] = lo
    outs = [pltpu.make_async_copy(mv, m_hbm, osem.at[0])]
    outs[0].start()
    w_z0.finish()
    w_y1.finish()
    outs.append(pltpu.make_async_copy(w, wo_hbm, osem.at[1]))
    outs[1].start()
    y_z0.finish()
    y_y1.finish()
    outs.append(pltpu.make_async_copy(y, y_hbm, osem.at[2]))
    outs[2].start()
    for copy in outs:
        copy.wait()
    links.drain()


COPIES = 180


def solve(t, wt, sc):
    return pl.pallas_call(
        solve_kernel,
        out_shape=[
            jax.ShapeDtypeStruct((2, 512, 768), B),
            jax.ShapeDtypeStruct((4, 384, 512), F),
            jax.ShapeDtypeStruct((4, 4, 48, 512), F),
        ],
        in_specs=[VMEM] * 3,
        out_specs=[ANY] * 3,
        scratch_shapes=[
            pltpu.VMEM((4, 64, 768), F),
            pltpu.VMEM((2, 32, 768), F),
            pltpu.VMEM((2, 64, 768), F),
            pltpu.VMEM((2, 4, 48, 256), F),
            pltpu.VMEM((4, 2, 48, 256), F),
            pltpu.VMEM((4, 4, 48, 256), F),
            pltpu.VMEM((4, 24, 256), F),
            pltpu.VMEM((4, 48, 256), F),
            pltpu.VMEM((2, 4, 8, 2, 8, 128), F),
            pltpu.VMEM((3, 8, 2, 8, 128), F),
            pltpu.VMEM((15, 4, 8, 128), F),
            pltpu.VMEM((8, 2, 8, 128), F),
            pltpu.VMEM((4, 8, 128), F),
            pltpu.VMEM((15, 8, 128), F),
            pltpu.VMEM((3, 8, 128), F),
            pltpu.VMEM((2, 2, 4, 8, 2, 8, 128), F),
            pltpu.VMEM((4, 2, 64, 768), F),
            pltpu.VMEM((384, 128), F),
            pltpu.VMEM((4, 384, 512), F),
            pltpu.VMEM((4, 4, 48, 512), F),
            pltpu.VMEM((512, 512), F),
            pltpu.VMEM((2, 512, 768), B),
            pltpu.SemaphoreType.DMA((COPIES,)),
            pltpu.SemaphoreType.DMA((COPIES,)),
            pltpu.SemaphoreType.DMA((3,)),
        ],
        compiler_params=pltpu.CompilerParams(vmem_limit_bytes=32 * MIB, collective_id=0, has_side_effects=True),
        name="solve",
    )(t.reshape(4, 2, 64, 768), wt.reshape(4, 4, 48, 512), sc)


def update_kernel(h_hbm, w_hbm, p_ref, m_hbm, y_hbm, wt_hbm, ho_hbm, wo_hbm, hv, wv, mm, yv, wt, sem, osem):
    col = lax.axis_index("col")
    count = [0]

    def fetch(src, dst):
        copy = pltpu.make_async_copy(src, dst, sem.at[count[0]])
        count[0] += 1
        copy.start()
        return copy

    def h_parts(block):
        hi, half = 1 - block // 2, block % 2
        starts = [384 * half + 128 * u for u in range(3)]
        return [(2 * (j // 256) + hi, j % 256) for j in starts]

    m_copies = [fetch(m_hbm.at[0], mm.at[pl.ds(0, 512)]), fetch(m_hbm.at[1], mm.at[pl.ds(512, 512)]),
                fetch(m_hbm.at[0], mm.at[pl.ds(1024, 512)])]
    loads = []
    for g in range(2):
        rows = pl.ds(384 * g, 384)
        loads.append([fetch(wt_hbm.at[rows], wt.at[rows])]
                     + [fetch(w_hbm.at[rows, b, 0, :], wv.at[rows, pl.ds(256 * b, 256)]) for b in range(3)])
    for block in range(4):
        copies = [fetch(y_hbm.at[block], yv.at[block])]
        for u, (a, j) in enumerate(h_parts(block)):
            rows = pl.ds(384 * block + 128 * u, 128)
            copies += [fetch(h_hbm.at[a, 0, pl.ds(j, 128), b, 0, :], hv.at[rows, pl.ds(256 * b, 256)]) for b in range(3)]
        loads.append(copies)
    cols = local_place(p_ref, 16, col)
    lane = lax.broadcasted_iota(jnp.int32, cols.shape, 1)
    hit = [jnp.max((cols == lane + 128 * q).astype(F), axis=0, keepdims=True) for q in range(6)]
    pruned_here = jnp.concatenate(hit, axis=1) > 0.5
    outs = []

    def put(src, dst):
        copy = pltpu.make_async_copy(src, dst, osem.at[len(outs)])
        copy.start()
        outs.append(copy)

    def product(left):
        hi, lo = split2(left)
        return dot(jnp.concatenate([hi, hi, lo], axis=1), mm[...], NN)

    for copy in m_copies:
        copy.wait()
    for g in range(2):
        for copy in loads[g]:
            copy.wait()
        rows = slice(384 * g, 384 * g + 384)
        wv[rows, :] = jnp.where(pruned_here, 0.0, wv[rows, :] - product(wt[rows, :]))
        for b in range(3):
            put(wv.at[pl.ds(384 * g, 384), pl.ds(256 * b, 256)], wo_hbm.at[pl.ds(384 * g, 384), b, 0, :])
    for block in range(4):
        for copy in loads[2 + block]:
            copy.wait()
        rows = slice(384 * block, 384 * block + 384)
        hv[rows, :] = hv[rows, :] - product(yv[block])
        for u, (a, j) in enumerate(h_parts(block)):
            for b in range(3):
                put(hv.at[pl.ds(384 * block + 128 * u, 128), pl.ds(256 * b, 256)], ho_hbm.at[a, 0, pl.ds(j, 128), b, 0, :])
    for copy in outs:
        copy.wait()


def update(hinverse, pruned, weights, m, y, wt):
    return pl.pallas_call(
        update_kernel,
        out_shape=[jax.ShapeDtypeStruct(hinverse.shape, F), jax.ShapeDtypeStruct(weights.shape, F)],
        in_specs=[ANY, ANY, VMEM, ANY, ANY, ANY],
        out_specs=[ANY, ANY],
        scratch_shapes=[
            pltpu.VMEM((1536, 768), F),
            pltpu.VMEM((768, 768), F),
            pltpu.VMEM((1536, 768), B),
            pltpu.VMEM((4, 384, 512), F),
            pltpu.VMEM((768, 512), F),
            pltpu.SemaphoreType.DMA((51,)),
            pltpu.SemaphoreType.DMA((42,)),
        ],
        compiler_params=pltpu.CompilerParams(vmem_limit_bytes=24 * MIB),
        name="update",
    )(hinverse, weights, pruned, m, y, wt)


def per_device(hinverse, pruned, weights):
    t, wt, sc = gather(hinverse, pruned, weights)
    m, y, w = solve(t, wt, sc)
    return update(hinverse, pruned, weights, m, y, w.reshape(768, 512))


def solution(mesh):
    placed = (P(None, "row", None, None, "col", None), P(), P("row", None, "col", None))
    return jax.shard_map(
        per_device,
        mesh=mesh,
        in_specs=placed,
        out_specs=(P(None, "row", None, None, "col", None), P("row", None, "col", None)),
        check_vma=False,
    )
```

```python
import jax
import jax.numpy as jnp
from jax import lax
from jax.experimental import pallas as pl
from jax.experimental.pallas import tpu as pltpu
from jax.sharding import PartitionSpec as P

F = jnp.float32
B = jnp.bfloat16
MESH = pl.DeviceIdType.MESH
HIGHEST = lax.Precision.HIGHEST
NN = ((1,), (0,))
NT = ((1,), (1,))
TN = ((0,), (0,))
HBM = pl.BlockSpec(memory_space=pltpu.HBM)
VMEM = pl.BlockSpec(memory_space=pltpu.VMEM)
MIB = 2**20


def split3(x):
    hi = x.astype(B)
    rest = x - hi.astype(F)
    mid = rest.astype(B)
    return hi, mid, (rest - mid.astype(F)).astype(B)


def split2(x):
    hi = x.astype(B)
    return hi, (x - hi.astype(F)).astype(B)


def dot(a, b, dims):
    return lax.dot_general(a, b, (dims, ((), ())), preferred_element_type=F)


def dot3(a, b, dims):
    (ah, al), (bh, bl) = a, b
    return dot(al, bh, dims) + dot(ah, bl, dims) + dot(ah, bh, dims)


def local_place(p_ref, parts, index):
    p = jnp.concatenate([p_ref[0:1, :], p_ref[1:2, :]], axis=1)
    p = jnp.broadcast_to(p, (128, p.shape[1])).T
    tile = p >> 8
    return jnp.where(tile % parts == index, (tile // parts) * 256 + (p & 255), -1)


def onehot(place, start, width):
    lane = lax.broadcasted_iota(jnp.int32, place.shape, 1)
    blocks = [(place == lane + (start + 128 * q)).astype(F).astype(B) for q in range(width // 128)]
    return jnp.concatenate(blocks, axis=1)


class Links:
    def __init__(self, send, recv):
        self.send, self.recv, self.count, self.started = send, recv, 0, []

    def copy(self, src, dst, device):
        n = self.count
        self.count += 1
        made = pltpu.make_async_remote_copy(
            src_ref=src, dst_ref=dst, send_sem=self.send.at[n], recv_sem=self.recv.at[n], device_id=device, device_id_type=MESH
        )
        made.start()
        self.started.append(made)
        return made

    def drain(self):
        for made in self.started:
            made.wait_send()


def halves_of(ref):
    n = ref.shape[0] // 2
    return ref.at[pl.ds(0, n)], ref.at[pl.ds(n, n)]


class RingSum:
    def __init__(self, links, i, up, down, full, boxes):
        self.links, self.i, self.up, self.down, self.full, self.boxes = links, i, up, down, full, boxes

    def start(self):
        left, right, left2, right2 = self.boxes
        far0, far1 = halves_of(self.full((self.i + 2) % 4))
        self.a = self.links.copy(far0, left, self.up)
        self.b = self.links.copy(far1, right, self.down)
        self.c = self.links.copy(halves_of(self.full((self.i + 1) % 4))[1], halves_of(left2)[1], self.up)
        self.d = self.links.copy(halves_of(self.full((self.i + 3) % 4))[0], halves_of(right2)[0], self.down)

    def near(self):
        left, right, left2, right2 = self.boxes
        self.a.wait_recv()
        part = halves_of(self.full((self.i + 1) % 4))[0]
        part[...] = part[...] + left[...]
        self.a = self.links.copy(part, halves_of(left2)[0], self.up)
        self.b.wait_recv()
        part = halves_of(self.full((self.i + 3) % 4))[1]
        part[...] = part[...] + right[...]
        self.b = self.links.copy(part, halves_of(right2)[1], self.down)

    def finish(self):
        _, _, left2, right2 = self.boxes
        for copy in (self.a, self.b, self.c, self.d):
            copy.wait_recv()
        return self.full(self.i)[...] + left2[...] + right2[...]


class RingGather:
    def __init__(self, links, i, up, down, full):
        self.links, self.i, self.up, self.down, self.full = links, i, up, down, full

    def own(self):
        first, second = halves_of(self.full(self.i))
        self.a = self.links.copy(first, first, self.up)
        self.b = self.links.copy(second, second, self.down)
        self.c = self.links.copy(second, second, self.up)
        self.d = self.links.copy(first, first, self.down)

    def forward(self):
        self.a.wait_recv()
        part = halves_of(self.full((self.i + 3) % 4))[0]
        self.a = self.links.copy(part, part, self.up)
        self.b.wait_recv()
        part = halves_of(self.full((self.i + 1) % 4))[1]
        self.b = self.links.copy(part, part, self.down)

    def finish(self):
        for copy in (self.a, self.b, self.c, self.d):
            copy.wait_recv()


def sweep8(groups, m):
    n = 8 * len(groups)
    row = groups[m]
    sub = lax.broadcasted_iota(jnp.int32, (8, n), 0)
    lane = lax.broadcasted_iota(jnp.int32, (8, n), 1)
    c = [jnp.broadcast_to(row[:, 8 * m + j : 8 * m + j + 1], (8, n)) for j in range(8)]
    for k in range(8):
        pivot = 1.0 / jnp.broadcast_to(c[k][k : k + 1, :], (8, n))
        at_k = sub == k
        ck = c[k]
        for j in range(8):
            if j != k:
                t = jnp.broadcast_to(c[j][k : k + 1, :], (8, n)) * pivot
                c[j] = jnp.where(at_k, t, c[j] - ck * t)
        c[k] = jnp.where(at_k, pivot, -(ck * pivot))
    inside = (lane >= 8 * m) & (lane < 8 * m + 8)
    row = jnp.where(inside, jnp.where(lane - 8 * m == sub, 1.0, 0.0), row)
    new = c[0] * jnp.broadcast_to(row[0:1, :], (8, n))
    for j in range(1, 8):
        new = new + c[j] * jnp.broadcast_to(row[j : j + 1, :], (8, n))
    spread = [jnp.broadcast_to(new[j : j + 1, :], (8, n)) for j in range(8)]
    out = []
    for i, group in enumerate(groups):
        if i == m:
            out.append(new)
            continue
        left = jnp.where(inside, 0.0, group)
        for j in range(8):
            left = left - jnp.broadcast_to(group[:, 8 * m + j : 8 * m + j + 1], (8, n)) * spread[j]
        out.append(left)
    return out


def fdot(a, b):
    return jnp.dot(a, b, precision=HIGHEST, preferred_element_type=F)


def invert128(block, between):
    groups = [block[8 * i : 8 * i + 8, :] for i in range(16)]
    for m in range(16):
        groups = sweep8(groups, m)
        if m % 4 == 3:
            between[m // 4]()
    return jnp.concatenate(groups, axis=0)


def invert_block(x, k, between):
    here = slice(128 * k, 128 * k + 128)
    inverse = invert128(x[here, here], between)
    row = fdot(inverse, x[here, :])
    column = x[:, here]
    x[...] = x[...] - fdot(column, row)
    x[:, here] = -fdot(column, inverse)
    x[here, :] = row
    x[here, here] = inverse


def gather_kernel(h_hbm, w_hbm, p_ref, t_ref, wt_ref, sc_ref, hv, wv, sem):
    row = lax.axis_index("row")
    col = lax.axis_index("col")
    w_copies, h_copies = [], []
    for b in range(3):
        copy = pltpu.make_async_copy(w_hbm.at[:, b, 0, :], wv.at[:, pl.ds(256 * b, 256)], sem.at[18 + b])
        copy.start()
        w_copies.append(copy)
    for a in range(6):
        for b in range(3):
            copy = pltpu.make_async_copy(
                h_hbm.at[a, 0, :, b, 0, :], hv.at[pl.ds(256 * a, 256), pl.ds(256 * b, 256)], sem.at[3 * a + b]
            )
            copy.start()
            h_copies.append(copy)
    cols = local_place(p_ref, 16, col)
    hot = [onehot(cols, 256 * b, 256) for b in range(3)]
    for b in range(3):
        w_copies[b].wait()
        hi, mid, lo = split3(wv[:, 256 * b : 256 * b + 256])
        part = dot(lo, hot[b], NT) + dot(mid, hot[b], NT) + dot(hi, hot[b], NT)
        wt_ref[...] = part if b == 0 else wt_ref[...] + part
    rows = local_place(p_ref, 8, row)
    for a in range(6):
        for copy in h_copies[3 * a : 3 * a + 3]:
            copy.wait()
        pick = onehot(rows, 256 * a, 256)
        hi, mid, lo = split3(hv[256 * a : 256 * a + 256, :])
        part = dot(pick, lo, NN) + dot(pick, mid, NN) + dot(pick, hi, NN)
        t_ref[...] = part if a == 0 else t_ref[...] + part
    total = None
    for b in range(3):
        hi, mid, lo = split3(t_ref[:, 256 * b : 256 * b + 256])
        part = dot(lo, hot[b], NT) + dot(mid, hot[b], NT) + dot(hi, hot[b], NT)
        total = part if b == 0 else total + part
    for v in range(2):
        for j in range(2):
            lanes = slice(256 * v + 128 * j, 256 * v + 128 * j + 128)
            sc_ref[:, v, :, :, j] = total[:, lanes].reshape(4, 2, 8, 8, 128).transpose(1, 0, 2, 3, 4)


def gather(hinverse, pruned, weights):
    return pl.pallas_call(
        gather_kernel,
        out_shape=[
            jax.ShapeDtypeStruct((512, 768), F),
            jax.ShapeDtypeStruct((768, 512), F),
            jax.ShapeDtypeStruct((2, 2, 4, 8, 2, 8, 128), F),
        ],
        in_specs=[HBM, HBM, VMEM],
        out_specs=[VMEM] * 3,
        scratch_shapes=[
            pltpu.VMEM((1536, 768), F),
            pltpu.VMEM((768, 768), F),
            pltpu.SemaphoreType.DMA((21,)),
        ],
        compiler_params=pltpu.CompilerParams(vmem_limit_bytes=48 * MIB),
        name="gather",
    )(hinverse, weights, pruned)


def solve_kernel(t, wt, sc, mv, y, w,
                 ra, xbox1, xbox2, wc, wboxf, wboxn, wbox2f, wbox2n,
                 sbox, px, qy, ps, qs, py, qx, sf, pan, ya, xs, send, recv):
    row = lax.axis_index("row")
    col = lax.axis_index("col")
    x, k = row // 2, row % 2
    z, yy = col // 4, col % 4
    cu, cl = col // 2, col % 2

    def dev(r, c):
        return {"row": r, "col": c}

    sibling = dev(2 * x + 1 - k, col)
    x_peers = [dev((row + 2 * d) % 8, col) for d in range(1, 4)]
    peers = [dev(row, (col + d) % 16) for d in range(1, 16)]
    x_up, x_down = x_peers[0], x_peers[2]
    y_up, y_down = dev(row, 4 * z + (yy + 1) % 4), dev(row, 4 * z + (yy + 3) % 4)
    z_up, z_down = peers[3], peers[11]
    target = dev(col % 8, 4 * (2 * (1 - col // 8) + k) + x)
    source = dev(2 * yy + z % 2, row + 8 * (1 - z // 2))

    barrier = pltpu.get_barrier_semaphore()
    greet = [sibling, target, source] + x_peers + peers
    for device in greet:
        pl.semaphore_signal(barrier, inc=1, device_id=device, device_id_type=MESH)
    pl.semaphore_wait(barrier, len(greet))
    links = Links(send, recv)

    first = [links.copy(sc.at[1 - k, v], sbox.at[v], sibling) for v in range(2)]
    order = [(x + 2) % 4, (x + 1) % 4, (x + 3) % 4, x]
    rows_in = [links.copy(t.at[j, 1 - k], ra.at[j], sibling) for j in order]

    lanes = [pl.ds(0, 256), pl.ds(256, 256)]
    sum_z0 = RingSum(links, z, z_up, z_down, lambda j: wt.at[j, :, :, lanes[0]],
                     (wboxf.at[0], wboxf.at[1], wboxn.at[0], wboxn.at[1]))
    sum_y1 = RingSum(links, yy, y_up, y_down, lambda j: wt.at[:, j, :, lanes[1]],
                     (wboxf.at[2], wboxf.at[3], wboxn.at[2], wboxn.at[3]))
    sum_y0 = RingSum(links, yy, y_up, y_down, lambda j: wc.at[0, j],
                     (wbox2f.at[0], wbox2f.at[1], wbox2n.at[0], wbox2n.at[1]))
    sum_z1 = RingSum(links, z, z_up, z_down, lambda j: wc.at[1, j],
                     (wbox2f.at[2], wbox2f.at[3], wbox2n.at[2], wbox2n.at[3]))
    sum_x = RingSum(links, x, x_up, x_down, lambda j: ra.at[j],
                    (xbox1.at[0], xbox1.at[1], xbox2.at[0], xbox2.at[1]))

    sum_z0.start()
    sum_y1.start()

    first[0].wait_recv()
    sbox[0] = sbox[0] + sc[k, 0]
    p1 = [links.copy(sbox.at[0, (x + d) % 4], px.at[d - 1], x_peers[d - 1]) for d in range(1, 4)]
    first[1].wait_recv()
    sbox[1] = sbox[1] + sc[k, 1]
    q1 = []
    for d in range(1, 16):
        q = (col + d) % 16
        q1.append(links.copy(sbox.at[1, :, q // 2, q % 2], qy.at[d - 1], peers[d - 1]))

    for n, j in enumerate(order):
        rows_in[n].wait_recv()
        ra[j] = ra[j] + t[j, k]
    sum_x.start()
    sum_z0.near()
    sum_y1.near()

    total = sbox[0, x]
    for d in range(1, 4):
        p1[d - 1].wait_recv()
        total = total + px[d - 1]
    ps[...] = total
    p2 = []
    for d in range(1, 16):
        q = (col + d) % 16
        p2.append(links.copy(ps.at[q // 2, q % 2], py.at[d - 1], peers[d - 1]))
    total = sbox[1, :, cu, cl]
    for d in range(1, 16):
        q1[d - 1].wait_recv()
        total = total + qy[d - 1]
    qs[...] = total
    q2 = [links.copy(qs.at[(x + d) % 4], qx.at[d - 1], x_peers[d - 1]) for d in range(1, 4)]

    sum_x.near()

    total = qs[x]
    for d in range(1, 4):
        q2[d - 1].wait_recv()
        total = total + qx[d - 1]
    own_q = sf.at[k, 1, x, cu, cl]
    own_q[...] = total
    q3 = [links.copy(own_q, own_q, x_peers[d - 1]) for d in range(1, 4)]
    total = ps[cu, cl]
    for d in range(1, 16):
        p2[d - 1].wait_recv()
        total = total + py[d - 1]
    own_p = sf.at[k, 0, x, cu, cl]
    own_p[...] = total
    p3 = [links.copy(own_p, own_p, peers[d - 1]) for d in range(1, 16)]

    wc[0] = sum_z0.finish()
    wc[1] = sum_y1.finish()
    sum_y0.start()
    sum_z1.start()

    for copy in q3:
        copy.wait_recv()
    own_q = sf.at[k, 1, :, cu, cl]
    q4 = [links.copy(own_q, own_q, peers[d - 1]) for d in range(1, 16)]
    for copy in p3:
        copy.wait_recv()
    own_p = sf.at[k, 0, x]
    p4 = [links.copy(own_p, own_p, x_peers[d - 1]) for d in range(1, 4)]

    pan[x, k] = sum_x.finish()
    mine = pan.at[x, k]
    paired = links.copy(mine, mine, sibling)
    sum_y0.near()
    sum_z1.near()

    paired.wait_recv()
    start = pl.multiple_of(384 * k, 128)
    ya[...] = pan[x, :, :, pl.ds(start, 384)].reshape(128, 384).T

    def lane_block(j):
        return pl.ds(pl.multiple_of(128 * j, 128), 128)

    moved = links.copy(ya, y.at[2 * (1 - col // 8) + k, :, lane_block(x)], target)

    w_y0 = RingGather(links, yy, y_up, y_down, lambda j: w.at[z, j, :, lanes[0]])
    w_z1 = RingGather(links, z, z_up, z_down, lambda j: w.at[j, yy, :, lanes[1]])
    w_z0 = RingGather(links, z, z_up, z_down, lambda j: w.at[j, :, :, lanes[0]])
    w_y1 = RingGather(links, yy, y_up, y_down, lambda j: w.at[:, j, :, lanes[1]])
    upper, lower = pl.ds(0, 192), pl.ds(192, 192)
    y_y0 = RingGather(links, yy, y_up, y_down, lambda j: y.at[z, upper, lane_block(j)])
    y_z1 = RingGather(links, z, z_up, z_down, lambda j: y.at[j, lower, lane_block(yy)])
    y_z0 = RingGather(links, z, z_up, z_down, lambda j: y.at[j, upper])
    y_y1 = RingGather(links, yy, y_up, y_down, lambda j: y.at[:, lower, lane_block(j)])
    pan_x = RingGather(links, x, x_up, x_down, lambda j: pan.at[j, k])
    w[z, yy, :, 0:256] = sum_y0.finish()
    w[z, yy, :, 256:512] = sum_z1.finish()
    w_y0.own()
    w_z1.own()

    for copy in q4 + p4:
        copy.wait_recv()
    own_s = sf.at[k]
    swap_s = links.copy(own_s, own_s, sibling)
    pan_x.own()
    w_y0.forward()
    w_z1.forward()
    moved.wait_recv()
    y_y0.own()
    y_z1.own()

    swap_s.wait_recv()
    for v in range(2):
        for j in range(2):
            xs[:, 256 * v + 128 * j : 256 * v + 128 * j + 128] = sf[:, v, :, :, j].transpose(1, 0, 2, 3, 4).reshape(512, 128)
    swaps = []

    def swap_panel():
        pan_x.finish()
        for n in range(1, 4):
            part = pan.at[(x + n) % 4, k]
            swaps.append(links.copy(part, part, sibling))

    def steps(*todo):
        def run():
            for step in todo:
                step()

        return run

    places = [
        steps(w_y0.finish, w_z1.finish, w_z0.own, w_y1.own),
        steps(y_y0.forward, y_z1.forward),
        steps(pan_x.forward, y_y0.finish, y_z0.own, y_z1.finish, y_y1.own),
        steps(),
        steps(swap_panel, w_z0.forward, w_y1.forward),
        steps(),
        steps(),
        steps(),
        steps(y_z0.forward, y_y1.forward),
    ]
    places += [steps()] * (16 - len(places))
    for n in range(4):
        invert_block(xs, n, places[4 * n : 4 * n + 4])
    for copy in swaps:
        copy.wait_recv()
    a = split2(xs[...])
    b = split2(pan[...].reshape(512, 768))
    hi, lo = split2(dot3(a, b, NN))
    mv[0] = hi
    mv[1] = lo
    w_z0.finish()
    w_y1.finish()
    y_z0.finish()
    y_y1.finish()
    links.drain()


COPIES = 180


def solve(t, wt, sc):
    return pl.pallas_call(
        solve_kernel,
        out_shape=[
            jax.ShapeDtypeStruct((2, 512, 768), B),
            jax.ShapeDtypeStruct((4, 384, 512), F),
            jax.ShapeDtypeStruct((4, 4, 48, 512), F),
        ],
        in_specs=[VMEM] * 3,
        out_specs=[VMEM] * 3,
        scratch_shapes=[
            pltpu.VMEM((4, 64, 768), F),
            pltpu.VMEM((2, 32, 768), F),
            pltpu.VMEM((2, 64, 768), F),
            pltpu.VMEM((2, 4, 48, 256), F),
            pltpu.VMEM((4, 2, 48, 256), F),
            pltpu.VMEM((4, 4, 48, 256), F),
            pltpu.VMEM((4, 24, 256), F),
            pltpu.VMEM((4, 48, 256), F),
            pltpu.VMEM((2, 4, 8, 2, 8, 128), F),
            pltpu.VMEM((3, 8, 2, 8, 128), F),
            pltpu.VMEM((15, 4, 8, 128), F),
            pltpu.VMEM((8, 2, 8, 128), F),
            pltpu.VMEM((4, 8, 128), F),
            pltpu.VMEM((15, 8, 128), F),
            pltpu.VMEM((3, 8, 128), F),
            pltpu.VMEM((2, 2, 4, 8, 2, 8, 128), F),
            pltpu.VMEM((4, 2, 64, 768), F),
            pltpu.VMEM((384, 128), F),
            pltpu.VMEM((512, 512), F),
            pltpu.SemaphoreType.DMA((COPIES,)),
            pltpu.SemaphoreType.DMA((COPIES,)),
        ],
        compiler_params=pltpu.CompilerParams(vmem_limit_bytes=32 * MIB, collective_id=0, has_side_effects=True),
        name="solve",
    )(t.reshape(4, 2, 64, 768), wt.reshape(4, 4, 48, 512), sc)


def update_kernel(h_hbm, w_hbm, p_ref, m, yv, wt, ho_hbm, wo_hbm, hv, wv, mm, sem, osem):
    col = lax.axis_index("col")
    count = [0]

    def fetch(src, dst):
        copy = pltpu.make_async_copy(src, dst, sem.at[count[0]])
        count[0] += 1
        copy.start()
        return copy

    def h_parts(block):
        hi, half = 1 - block // 2, block % 2
        starts = [384 * half + 128 * u for u in range(3)]
        return [(2 * (j // 256) + hi, j % 256) for j in starts]

    loads = []
    for g in range(2):
        rows = pl.ds(384 * g, 384)
        loads.append([fetch(w_hbm.at[rows, b, 0, :], wv.at[rows, pl.ds(256 * b, 256)]) for b in range(3)])
    for block in range(4):
        copies = []
        for u, (a, j) in enumerate(h_parts(block)):
            rows = pl.ds(384 * block + 128 * u, 128)
            copies += [fetch(h_hbm.at[a, 0, pl.ds(j, 128), b, 0, :], hv.at[rows, pl.ds(256 * b, 256)]) for b in range(3)]
        loads.append(copies)
    cols = local_place(p_ref, 16, col)
    lane = lax.broadcasted_iota(jnp.int32, cols.shape, 1)
    hit = [jnp.max((cols == lane + 128 * q).astype(F), axis=0, keepdims=True) for q in range(6)]
    pruned_here = jnp.concatenate(hit, axis=1) > 0.5
    outs = []

    def put(src, dst):
        copy = pltpu.make_async_copy(src, dst, osem.at[len(outs)])
        copy.start()
        outs.append(copy)

    def product(left):
        hi, lo = split2(left)
        return dot(jnp.concatenate([hi, hi, lo], axis=1), mm[...], NN)

    mm[0:512, :] = m[0]
    mm[512:1024, :] = m[1]
    mm[1024:1536, :] = m[0]
    for g in range(2):
        for copy in loads[g]:
            copy.wait()
        rows = slice(384 * g, 384 * g + 384)
        wv[rows, :] = jnp.where(pruned_here, 0.0, wv[rows, :] - product(wt[rows, :]))
        for b in range(3):
            put(wv.at[pl.ds(384 * g, 384), pl.ds(256 * b, 256)], wo_hbm.at[pl.ds(384 * g, 384), b, 0, :])
    for block in range(4):
        for copy in loads[2 + block]:
            copy.wait()
        rows = slice(384 * block, 384 * block + 384)
        hv[rows, :] = hv[rows, :] - product(yv[block])
        for u, (a, j) in enumerate(h_parts(block)):
            for b in range(3):
                put(hv.at[pl.ds(384 * block + 128 * u, 128), pl.ds(256 * b, 256)], ho_hbm.at[a, 0, pl.ds(j, 128), b, 0, :])
    for copy in outs:
        copy.wait()


def update(hinverse, pruned, weights, m, y, wt):
    return pl.pallas_call(
        update_kernel,
        out_shape=[jax.ShapeDtypeStruct(hinverse.shape, F), jax.ShapeDtypeStruct(weights.shape, F)],
        in_specs=[HBM, HBM, VMEM, VMEM, VMEM, VMEM],
        out_specs=[HBM, HBM],
        scratch_shapes=[
            pltpu.VMEM((1536, 768), F),
            pltpu.VMEM((768, 768), F),
            pltpu.VMEM((1536, 768), B),
            pltpu.SemaphoreType.DMA((42,)),
            pltpu.SemaphoreType.DMA((42,)),
        ],
        compiler_params=pltpu.CompilerParams(vmem_limit_bytes=44 * MIB),
        name="update",
    )(hinverse, weights, pruned, m, y, wt)


def per_device(hinverse, pruned, weights):
    t, wt, sc = gather(hinverse, pruned, weights)
    m, y, w = solve(t, wt, sc)
    return update(hinverse, pruned, weights, m, y, w.reshape(768, 512))


def solution(mesh):
    placed = (P(None, "row", None, None, "col", None), P(), P("row", None, "col", None))
    return jax.shard_map(
        per_device,
        mesh=mesh,
        in_specs=placed,
        out_specs=(P(None, "row", None, None, "col", None), P("row", None, "col", None)),
        check_vma=False,
    )
```

```python
import jax
import jax.numpy as jnp
from jax import lax
from jax.experimental import pallas as pl
from jax.experimental.pallas import tpu as pltpu
from jax.sharding import PartitionSpec as P

F = jnp.float32
B = jnp.bfloat16
MESH = pl.DeviceIdType.MESH
HIGHEST = lax.Precision.HIGHEST
NN = ((1,), (0,))
NT = ((1,), (1,))
TN = ((0,), (0,))
HBM = pl.BlockSpec(memory_space=pltpu.HBM)
VMEM = pl.BlockSpec(memory_space=pltpu.VMEM)
MIB = 2**20


def split3(x):
    hi = x.astype(B)
    rest = x - hi.astype(F)
    mid = rest.astype(B)
    return hi, mid, (rest - mid.astype(F)).astype(B)


def split2(x):
    hi = x.astype(B)
    return hi, (x - hi.astype(F)).astype(B)


def dot(a, b, dims):
    return lax.dot_general(a, b, (dims, ((), ())), preferred_element_type=F)


def dot3(a, b, dims):
    (ah, al), (bh, bl) = a, b
    return dot(al, bh, dims) + dot(ah, bl, dims) + dot(ah, bh, dims)


def local_place(p_ref, parts, index):
    p = jnp.concatenate([p_ref[0:1, :], p_ref[1:2, :]], axis=1)
    p = jnp.broadcast_to(p, (128, p.shape[1])).T
    tile = p >> 8
    return jnp.where(tile % parts == index, (tile // parts) * 256 + (p & 255), -1)


def onehot(place, start, width):
    lane = lax.broadcasted_iota(jnp.int32, place.shape, 1)
    blocks = [(place == lane + (start + 128 * q)).astype(F).astype(B) for q in range(width // 128)]
    return jnp.concatenate(blocks, axis=1)


class Links:
    def __init__(self, send, recv):
        self.send, self.recv, self.count, self.started = send, recv, 0, []

    def copy(self, src, dst, device):
        n = self.count
        self.count += 1
        made = pltpu.make_async_remote_copy(
            src_ref=src, dst_ref=dst, send_sem=self.send.at[n], recv_sem=self.recv.at[n], device_id=device, device_id_type=MESH
        )
        made.start()
        self.started.append(made)
        return made

    def drain(self):
        for made in self.started:
            made.wait_send()


def halves_of(ref):
    n = ref.shape[0] // 2
    return ref.at[pl.ds(0, n)], ref.at[pl.ds(n, n)]


class RingSum:
    def __init__(self, links, i, up, down, full, boxes):
        self.links, self.i, self.up, self.down, self.full, self.boxes = links, i, up, down, full, boxes

    def start(self):
        left, right, left2, right2 = self.boxes
        far0, far1 = halves_of(self.full((self.i + 2) % 4))
        self.a = self.links.copy(far0, left, self.up)
        self.b = self.links.copy(far1, right, self.down)
        self.c = self.links.copy(halves_of(self.full((self.i + 1) % 4))[1], halves_of(left2)[1], self.up)
        self.d = self.links.copy(halves_of(self.full((self.i + 3) % 4))[0], halves_of(right2)[0], self.down)

    def near(self):
        left, right, left2, right2 = self.boxes
        self.a.wait_recv()
        part = halves_of(self.full((self.i + 1) % 4))[0]
        part[...] = part[...] + left[...]
        self.a = self.links.copy(part, halves_of(left2)[0], self.up)
        self.b.wait_recv()
        part = halves_of(self.full((self.i + 3) % 4))[1]
        part[...] = part[...] + right[...]
        self.b = self.links.copy(part, halves_of(right2)[1], self.down)

    def finish(self):
        _, _, left2, right2 = self.boxes
        for copy in (self.a, self.b, self.c, self.d):
            copy.wait_recv()
        return self.full(self.i)[...] + left2[...] + right2[...]


class RingGather:
    def __init__(self, links, i, up, down, full):
        self.links, self.i, self.up, self.down, self.full = links, i, up, down, full

    def own(self):
        first, second = halves_of(self.full(self.i))
        self.a = self.links.copy(first, first, self.up)
        self.b = self.links.copy(second, second, self.down)
        self.c = self.links.copy(second, second, self.up)
        self.d = self.links.copy(first, first, self.down)

    def forward(self):
        self.a.wait_recv()
        part = halves_of(self.full((self.i + 3) % 4))[0]
        self.a = self.links.copy(part, part, self.up)
        self.b.wait_recv()
        part = halves_of(self.full((self.i + 1) % 4))[1]
        self.b = self.links.copy(part, part, self.down)

    def finish(self):
        for copy in (self.a, self.b, self.c, self.d):
            copy.wait_recv()


def sweep8(groups, m):
    n = 8 * len(groups)
    row = groups[m]
    sub = lax.broadcasted_iota(jnp.int32, (8, n), 0)
    lane = lax.broadcasted_iota(jnp.int32, (8, n), 1)
    c = [jnp.broadcast_to(row[:, 8 * m + j : 8 * m + j + 1], (8, n)) for j in range(8)]
    for k in range(8):
        pivot = 1.0 / jnp.broadcast_to(c[k][k : k + 1, :], (8, n))
        at_k = sub == k
        ck = c[k]
        for j in range(8):
            if j != k:
                t = jnp.broadcast_to(c[j][k : k + 1, :], (8, n)) * pivot
                c[j] = jnp.where(at_k, t, c[j] - ck * t)
        c[k] = jnp.where(at_k, pivot, -(ck * pivot))
    inside = (lane >= 8 * m) & (lane < 8 * m + 8)
    row = jnp.where(inside, jnp.where(lane - 8 * m == sub, 1.0, 0.0), row)
    new = c[0] * jnp.broadcast_to(row[0:1, :], (8, n))
    for j in range(1, 8):
        new = new + c[j] * jnp.broadcast_to(row[j : j + 1, :], (8, n))
    spread = [jnp.broadcast_to(new[j : j + 1, :], (8, n)) for j in range(8)]
    out = []
    for i, group in enumerate(groups):
        if i == m:
            out.append(new)
            continue
        left = jnp.where(inside, 0.0, group)
        for j in range(8):
            left = left - jnp.broadcast_to(group[:, 8 * m + j : 8 * m + j + 1], (8, n)) * spread[j]
        out.append(left)
    return out


def fdot(a, b):
    return jnp.dot(a, b, precision=HIGHEST, preferred_element_type=F)


def invert128(block, between):
    groups = [block[8 * i : 8 * i + 8, :] for i in range(16)]
    for m in range(16):
        groups = sweep8(groups, m)
        if m % 4 == 3:
            between[m // 4]()
    return jnp.concatenate(groups, axis=0)


def invert_block(x, k, between):
    here = slice(128 * k, 128 * k + 128)
    inverse = invert128(x[here, here], between)
    row = fdot(inverse, x[here, :])
    column = x[:, here]
    x[...] = x[...] - fdot(column, row)
    x[:, here] = -fdot(column, inverse)
    x[here, :] = row
    x[here, here] = inverse


def gather_kernel(h_hbm, w_hbm, p_ref, t_ref, wt_ref, sc_ref, hv, wv, sem):
    row = lax.axis_index("row")
    col = lax.axis_index("col")
    w_copies, h_copies = [], []
    for b in range(3):
        copy = pltpu.make_async_copy(w_hbm.at[:, b, 0, :], wv.at[:, pl.ds(256 * b, 256)], sem.at[18 + b])
        copy.start()
        w_copies.append(copy)
    for a in range(6):
        for b in range(3):
            copy = pltpu.make_async_copy(
                h_hbm.at[a, 0, :, b, 0, :], hv.at[pl.ds(256 * a, 256), pl.ds(256 * b, 256)], sem.at[3 * a + b]
            )
            copy.start()
            h_copies.append(copy)
    cols = local_place(p_ref, 16, col)
    hot = [onehot(cols, 256 * b, 256) for b in range(3)]
    for b in range(3):
        w_copies[b].wait()
        hi, mid, lo = split3(wv[:, 256 * b : 256 * b + 256])
        part = dot(lo, hot[b], NT) + dot(mid, hot[b], NT) + dot(hi, hot[b], NT)
        wt_ref[...] = part if b == 0 else wt_ref[...] + part
    rows = local_place(p_ref, 8, row)
    for a in range(6):
        for copy in h_copies[3 * a : 3 * a + 3]:
            copy.wait()
        pick = onehot(rows, 256 * a, 256)
        hi, mid, lo = split3(hv[256 * a : 256 * a + 256, :])
        part = dot(pick, lo, NN) + dot(pick, mid, NN) + dot(pick, hi, NN)
        t_ref[...] = part if a == 0 else t_ref[...] + part
    total = None
    for b in range(3):
        hi, mid, lo = split3(t_ref[:, 256 * b : 256 * b + 256])
        part = dot(lo, hot[b], NT) + dot(mid, hot[b], NT) + dot(hi, hot[b], NT)
        total = part if b == 0 else total + part
    for v in range(2):
        for j in range(2):
            lanes = slice(256 * v + 128 * j, 256 * v + 128 * j + 128)
            sc_ref[:, v, :, :, j] = total[:, lanes].reshape(4, 2, 8, 8, 128).transpose(1, 0, 2, 3, 4)


def gather(hinverse, pruned, weights):
    return pl.pallas_call(
        gather_kernel,
        out_shape=[
            jax.ShapeDtypeStruct((512, 768), F),
            jax.ShapeDtypeStruct((768, 512), F),
            jax.ShapeDtypeStruct((2, 2, 4, 8, 2, 8, 128), F),
            jax.ShapeDtypeStruct((1536, 768), F),
            jax.ShapeDtypeStruct((768, 768), F),
        ],
        in_specs=[HBM, HBM, VMEM],
        out_specs=[VMEM] * 5,
        scratch_shapes=[pltpu.SemaphoreType.DMA((21,))],
        compiler_params=pltpu.CompilerParams(vmem_limit_bytes=40 * MIB),
        name="gather",
    )(hinverse, weights, pruned)


def solve_kernel(t, wt, sc, mv, y, w,
                 ra, xbox1, xbox2, wc, wboxf, wboxn, wbox2f, wbox2n,
                 sbox, px, qy, ps, qs, py, qx, sf, pan, ya, xs, send, recv):
    row = lax.axis_index("row")
    col = lax.axis_index("col")
    x, k = row // 2, row % 2
    z, yy = col // 4, col % 4
    cu, cl = col // 2, col % 2

    def dev(r, c):
        return {"row": r, "col": c}

    sibling = dev(2 * x + 1 - k, col)
    x_peers = [dev((row + 2 * d) % 8, col) for d in range(1, 4)]
    peers = [dev(row, (col + d) % 16) for d in range(1, 16)]
    x_up, x_down = x_peers[0], x_peers[2]
    y_up, y_down = dev(row, 4 * z + (yy + 1) % 4), dev(row, 4 * z + (yy + 3) % 4)
    z_up, z_down = peers[3], peers[11]
    target = dev(col % 8, 4 * (2 * (1 - col // 8) + k) + x)
    source = dev(2 * yy + z % 2, row + 8 * (1 - z // 2))

    barrier = pltpu.get_barrier_semaphore()
    greet = [sibling, target, source] + x_peers + peers
    for device in greet:
        pl.semaphore_signal(barrier, inc=1, device_id=device, device_id_type=MESH)
    pl.semaphore_wait(barrier, len(greet))
    links = Links(send, recv)

    first = [links.copy(sc.at[1 - k, v], sbox.at[v], sibling) for v in range(2)]
    order = [(x + 2) % 4, (x + 1) % 4, (x + 3) % 4, x]

    def half_columns(core):
        return pl.ds(pl.multiple_of(384 * core, 128), 384)

    rows_in = [links.copy(t.at[j, :, half_columns(1 - k)], ra.at[j], sibling) for j in order]

    lanes = [pl.ds(0, 256), pl.ds(256, 256)]
    sum_z0 = RingSum(links, z, z_up, z_down, lambda j: wt.at[j, :, :, lanes[0]],
                     (wboxf.at[0], wboxf.at[1], wboxn.at[0], wboxn.at[1]))
    sum_y1 = RingSum(links, yy, y_up, y_down, lambda j: wt.at[:, j, :, lanes[1]],
                     (wboxf.at[2], wboxf.at[3], wboxn.at[2], wboxn.at[3]))
    sum_y0 = RingSum(links, yy, y_up, y_down, lambda j: wc.at[0, j],
                     (wbox2f.at[0], wbox2f.at[1], wbox2n.at[0], wbox2n.at[1]))
    sum_z1 = RingSum(links, z, z_up, z_down, lambda j: wc.at[1, j],
                     (wbox2f.at[2], wbox2f.at[3], wbox2n.at[2], wbox2n.at[3]))
    sum_x = RingSum(links, x, x_up, x_down, lambda j: ra.at[j],
                    (xbox1.at[0], xbox1.at[1], xbox2.at[0], xbox2.at[1]))

    sum_z0.start()
    sum_y1.start()

    first[0].wait_recv()
    sbox[0] = sbox[0] + sc[k, 0]
    p1 = [links.copy(sbox.at[0, (x + d) % 4], px.at[d - 1], x_peers[d - 1]) for d in range(1, 4)]
    first[1].wait_recv()
    sbox[1] = sbox[1] + sc[k, 1]
    q1 = []
    for d in range(1, 16):
        q = (col + d) % 16
        q1.append(links.copy(sbox.at[1, :, q // 2, q % 2], qy.at[d - 1], peers[d - 1]))

    for n, j in enumerate(order):
        rows_in[n].wait_recv()
        ra[j] = ra[j] + t[j, :, half_columns(k)]
    sum_x.start()
    sum_z0.near()
    sum_y1.near()

    total = sbox[0, x]
    for d in range(1, 4):
        p1[d - 1].wait_recv()
        total = total + px[d - 1]
    ps[...] = total
    p2 = []
    for d in range(1, 16):
        q = (col + d) % 16
        p2.append(links.copy(ps.at[q // 2, q % 2], py.at[d - 1], peers[d - 1]))
    total = sbox[1, :, cu, cl]
    for d in range(1, 16):
        q1[d - 1].wait_recv()
        total = total + qy[d - 1]
    qs[...] = total
    q2 = [links.copy(qs.at[(x + d) % 4], qx.at[d - 1], x_peers[d - 1]) for d in range(1, 4)]

    sum_x.near()

    total = qs[x]
    for d in range(1, 4):
        q2[d - 1].wait_recv()
        total = total + qx[d - 1]
    own_q = sf.at[k, 1, x, cu, cl]
    own_q[...] = total
    q3 = [links.copy(own_q, own_q, x_peers[d - 1]) for d in range(1, 4)]
    total = ps[cu, cl]
    for d in range(1, 16):
        p2[d - 1].wait_recv()
        total = total + py[d - 1]
    own_p = sf.at[k, 0, x, cu, cl]
    own_p[...] = total
    p3 = [links.copy(own_p, own_p, peers[d - 1]) for d in range(1, 16)]

    piece = sum_x.finish()
    pan[x, :, half_columns(k)] = piece
    ya[...] = piece.T

    def lane_block(j):
        return pl.ds(pl.multiple_of(128 * j, 128), 128)

    moved = links.copy(ya, y.at[2 * (1 - col // 8) + k, :, lane_block(x)], target)

    for copy in q3:
        copy.wait_recv()
    own_q = sf.at[k, 1, :, cu, cl]
    q4 = [links.copy(own_q, own_q, peers[d - 1]) for d in range(1, 16)]
    for copy in p3:
        copy.wait_recv()
    own_p = sf.at[k, 0, x]
    p4 = [links.copy(own_p, own_p, x_peers[d - 1]) for d in range(1, 4)]

    wc[0] = sum_z0.finish()
    wc[1] = sum_y1.finish()
    sum_y0.start()
    sum_z1.start()

    w_y0 = RingGather(links, yy, y_up, y_down, lambda j: w.at[z, j, :, lanes[0]])
    w_z1 = RingGather(links, z, z_up, z_down, lambda j: w.at[j, yy, :, lanes[1]])
    w_z0 = RingGather(links, z, z_up, z_down, lambda j: w.at[j, :, :, lanes[0]])
    w_y1 = RingGather(links, yy, y_up, y_down, lambda j: w.at[:, j, :, lanes[1]])
    upper, lower = pl.ds(0, 192), pl.ds(192, 192)
    y_y0 = RingGather(links, yy, y_up, y_down, lambda j: y.at[z, upper, lane_block(j)])
    y_z1 = RingGather(links, z, z_up, z_down, lambda j: y.at[j, lower, lane_block(yy)])
    y_z0 = RingGather(links, z, z_up, z_down, lambda j: y.at[j, upper])
    y_y1 = RingGather(links, yy, y_up, y_down, lambda j: y.at[:, lower, lane_block(j)])
    pan_x = RingGather(links, x, x_up, x_down, lambda j: pan.at[j, :, half_columns(k)])

    for copy in q4 + p4:
        copy.wait_recv()
    own_s = sf.at[k]
    swap_s = links.copy(own_s, own_s, sibling)
    pan_x.own()
    sum_y0.near()
    sum_z1.near()
    swap_s.wait_recv()
    for v in range(2):
        for j in range(2):
            xs[:, 256 * v + 128 * j : 256 * v + 128 * j + 128] = sf[:, v, :, :, j].transpose(1, 0, 2, 3, 4).reshape(512, 128)

    swaps = []

    def start_columns():
        moved.wait_recv()
        y_y0.own()
        y_z1.own()

    def start_weights():
        w[z, yy, :, 0:256] = sum_y0.finish()
        w[z, yy, :, 256:512] = sum_z1.finish()
        w_y0.own()
        w_z1.own()

    def swap_panel():
        pan_x.finish()
        for n in range(4):
            part = pan.at[(x + n) % 4, :, half_columns(k)]
            swaps.append(links.copy(part, part, sibling))

    def steps(*todo):
        def run():
            for step in todo:
                step()

        return run

    places = [
        steps(start_columns),
        steps(start_weights),
        steps(y_y0.forward, y_z1.forward),
        steps(w_y0.forward, w_z1.forward, pan_x.forward),
        steps(y_y0.finish, y_z0.own, y_z1.finish, y_y1.own),
        steps(w_y0.finish, w_z1.finish, w_z0.own, w_y1.own),
        steps(swap_panel),
        steps(),
        steps(y_z0.forward, y_y1.forward),
        steps(),
        steps(w_z0.forward, w_y1.forward),
    ]
    places += [steps()] * (16 - len(places))
    for n in range(4):
        invert_block(xs, n, places[4 * n : 4 * n + 4])
    for copy in swaps:
        copy.wait_recv()
    a = split2(xs[...])
    b = split2(pan[...].reshape(512, 768))
    hi, lo = split2(dot3(a, b, NN))
    mv[0:512, :] = hi
    mv[512:1024, :] = lo
    mv[1024:1536, :] = hi
    w_z0.finish()
    w_y1.finish()
    y_z0.finish()
    y_y1.finish()
    links.drain()


COPIES = 180


def solve(t, wt, sc):
    return pl.pallas_call(
        solve_kernel,
        out_shape=[
            jax.ShapeDtypeStruct((1536, 768), B),
            jax.ShapeDtypeStruct((4, 384, 512), F),
            jax.ShapeDtypeStruct((4, 4, 48, 512), F),
        ],
        in_specs=[VMEM] * 3,
        out_specs=[VMEM] * 3,
        scratch_shapes=[
            pltpu.VMEM((4, 128, 384), F),
            pltpu.VMEM((2, 64, 384), F),
            pltpu.VMEM((2, 128, 384), F),
            pltpu.VMEM((2, 4, 48, 256), F),
            pltpu.VMEM((4, 2, 48, 256), F),
            pltpu.VMEM((4, 4, 48, 256), F),
            pltpu.VMEM((4, 24, 256), F),
            pltpu.VMEM((4, 48, 256), F),
            pltpu.VMEM((2, 4, 8, 2, 8, 128), F),
            pltpu.VMEM((3, 8, 2, 8, 128), F),
            pltpu.VMEM((15, 4, 8, 128), F),
            pltpu.VMEM((8, 2, 8, 128), F),
            pltpu.VMEM((4, 8, 128), F),
            pltpu.VMEM((15, 8, 128), F),
            pltpu.VMEM((3, 8, 128), F),
            pltpu.VMEM((2, 2, 4, 8, 2, 8, 128), F),
            pltpu.VMEM((4, 128, 768), F),
            pltpu.VMEM((384, 128), F),
            pltpu.VMEM((512, 512), F),
            pltpu.SemaphoreType.DMA((COPIES,)),
            pltpu.SemaphoreType.DMA((COPIES,)),
        ],
        compiler_params=pltpu.CompilerParams(vmem_limit_bytes=32 * MIB, collective_id=0, has_side_effects=True),
        name="solve",
    )(t.reshape(4, 128, 768), wt.reshape(4, 4, 48, 512), sc)


def update_kernel(hv, wv, p_ref, mm, yv, wt, ho_hbm, wo_hbm, hn, wn, osem):
    col = lax.axis_index("col")
    cols = local_place(p_ref, 16, col)
    lane = lax.broadcasted_iota(jnp.int32, cols.shape, 1)
    hit = [jnp.max((cols == lane + 128 * q).astype(F), axis=0, keepdims=True) for q in range(6)]
    pruned_here = jnp.concatenate(hit, axis=1) > 0.5
    outs = []

    def put(src, dst):
        copy = pltpu.make_async_copy(src, dst, osem.at[len(outs)])
        copy.start()
        outs.append(copy)

    def product(left):
        hi, lo = split2(left)
        return dot(jnp.concatenate([hi, hi, lo], axis=1), mm[...], NN)

    for block in range(4):
        hi, half = 1 - block // 2, block % 2
        runs = [(2 * (j // 256) + hi, j % 256) for j in (384 * half, 384 * half + 128, 384 * half + 256)]
        change = product(yv[block])
        for u, (a, j) in enumerate(runs):
            here = slice(256 * a + j, 256 * a + j + 128)
            hn[here, :] = hv[here, :] - change[128 * u : 128 * u + 128, :]
            for b in range(3):
                put(hn.at[pl.ds(256 * a + j, 128), pl.ds(256 * b, 256)], ho_hbm.at[a, 0, pl.ds(j, 128), b, 0, :])
    for g in range(2):
        rows = slice(384 * g, 384 * g + 384)
        wn[rows, :] = jnp.where(pruned_here, 0.0, wv[rows, :] - product(wt[rows, :]))
        for b in range(3):
            put(wn.at[pl.ds(384 * g, 384), pl.ds(256 * b, 256)], wo_hbm.at[pl.ds(384 * g, 384), b, 0, :])
    for copy in outs:
        copy.wait()


def update(hinverse, pruned, weights, hv, wv, m, y, wt):
    return pl.pallas_call(
        update_kernel,
        out_shape=[jax.ShapeDtypeStruct(hinverse.shape, F), jax.ShapeDtypeStruct(weights.shape, F)],
        in_specs=[VMEM] * 6,
        out_specs=[HBM, HBM],
        scratch_shapes=[
            pltpu.VMEM((1536, 768), F),
            pltpu.VMEM((768, 768), F),
            pltpu.SemaphoreType.DMA((42,)),
        ],
        compiler_params=pltpu.CompilerParams(vmem_limit_bytes=36 * MIB),
        name="update",
    )(hv, wv, pruned, m, y, wt)


def per_device(hinverse, pruned, weights):
    t, wt, sc, hv, wv = gather(hinverse, pruned, weights)
    m, y, w = solve(t, wt, sc)
    return update(hinverse, pruned, weights, hv, wv, m, y, w.reshape(768, 512))


def solution(mesh):
    placed = (P(None, "row", None, None, "col", None), P(), P("row", None, "col", None))
    return jax.shard_map(
        per_device,
        mesh=mesh,
        in_specs=placed,
        out_specs=(P(None, "row", None, None, "col", None), P("row", None, "col", None)),
        check_vma=False,
    )
```

```python
import jax
import jax.numpy as jnp
from jax import lax
from jax.experimental import pallas as pl
from jax.experimental.pallas import tpu as pltpu
from jax.sharding import PartitionSpec as P

F = jnp.float32
B = jnp.bfloat16
MESH = pl.DeviceIdType.MESH
HIGHEST = lax.Precision.HIGHEST
NN = ((1,), (0,))
NT = ((1,), (1,))
TN = ((0,), (0,))
HBM = pl.BlockSpec(memory_space=pltpu.HBM)
VMEM = pl.BlockSpec(memory_space=pltpu.VMEM)
MIB = 2**20


def split3(x, axis):
    hi = x.astype(B)
    rest = x - hi.astype(F)
    mid = rest.astype(B)
    return jnp.concatenate([(rest - mid.astype(F)).astype(B), mid, hi], axis=axis)


def split2(x):
    hi = x.astype(B)
    return hi, (x - hi.astype(F)).astype(B)


def dot(a, b, dims):
    return lax.dot_general(a, b, (dims, ((), ())), preferred_element_type=F)


def local_place(p_ref, parts, index):
    p = jnp.concatenate([p_ref[0:1, :], p_ref[1:2, :]], axis=1)
    p = jnp.broadcast_to(p, (128, p.shape[1])).T
    tile = p >> 8
    return jnp.where(tile % parts == index, (tile // parts) * 256 + (p & 255), -1)


def onehot(place, start, width):
    lane = lax.broadcasted_iota(jnp.int32, place.shape, 1)
    blocks = [(place == lane + (start + 128 * q)).astype(F).astype(B) for q in range(width // 128)]
    return jnp.concatenate(blocks, axis=1)


class Links:
    def __init__(self, send, recv):
        self.send, self.recv, self.count, self.started = send, recv, 0, []

    def copy(self, src, dst, device):
        n = self.count
        self.count += 1
        made = pltpu.make_async_remote_copy(
            src_ref=src, dst_ref=dst, send_sem=self.send.at[n], recv_sem=self.recv.at[n], device_id=device, device_id_type=MESH
        )
        made.start()
        self.started.append(made)
        return made

    def drain(self):
        for made in self.started:
            made.wait_send()


def halves_of(ref):
    n = ref.shape[0] // 2
    return ref.at[pl.ds(0, n)], ref.at[pl.ds(n, n)]


class RingSum:
    def __init__(self, links, i, up, down, full, boxes):
        self.links, self.i, self.up, self.down, self.full, self.boxes = links, i, up, down, full, boxes

    def start(self):
        left, right, left2, right2 = self.boxes
        far0, far1 = halves_of(self.full((self.i + 2) % 4))
        self.a = self.links.copy(far0, left, self.up)
        self.b = self.links.copy(far1, right, self.down)
        self.c = self.links.copy(halves_of(self.full((self.i + 1) % 4))[1], halves_of(left2)[1], self.up)
        self.d = self.links.copy(halves_of(self.full((self.i + 3) % 4))[0], halves_of(right2)[0], self.down)

    def near(self):
        left, right, left2, right2 = self.boxes
        self.a.wait_recv()
        part = halves_of(self.full((self.i + 1) % 4))[0]
        part[...] = part[...] + left[...]
        self.a = self.links.copy(part, halves_of(left2)[0], self.up)
        self.b.wait_recv()
        part = halves_of(self.full((self.i + 3) % 4))[1]
        part[...] = part[...] + right[...]
        self.b = self.links.copy(part, halves_of(right2)[1], self.down)

    def finish(self):
        _, _, left2, right2 = self.boxes
        for copy in (self.a, self.b, self.c, self.d):
            copy.wait_recv()
        return self.full(self.i)[...] + left2[...] + right2[...]


class RingGather:
    def __init__(self, links, i, up, down, full):
        self.links, self.i, self.up, self.down, self.full = links, i, up, down, full

    def own(self):
        first, second = halves_of(self.full(self.i))
        self.a = self.links.copy(first, first, self.up)
        self.b = self.links.copy(second, second, self.down)
        self.c = self.links.copy(second, second, self.up)
        self.d = self.links.copy(first, first, self.down)

    def forward(self):
        self.a.wait_recv()
        part = halves_of(self.full((self.i + 3) % 4))[0]
        self.a = self.links.copy(part, part, self.up)
        self.b.wait_recv()
        part = halves_of(self.full((self.i + 1) % 4))[1]
        self.b = self.links.copy(part, part, self.down)

    def finish(self):
        for copy in (self.a, self.b, self.c, self.d):
            copy.wait_recv()


def sweep8(groups, m):
    n = 8 * len(groups)
    row = groups[m]
    sub = lax.broadcasted_iota(jnp.int32, (8, n), 0)
    lane = lax.broadcasted_iota(jnp.int32, (8, n), 1)
    c = [jnp.broadcast_to(row[:, 8 * m + j : 8 * m + j + 1], (8, n)) for j in range(8)]
    for k in range(8):
        pivot = 1.0 / jnp.broadcast_to(c[k][k : k + 1, :], (8, n))
        at_k = sub == k
        ck = c[k]
        for j in range(8):
            if j != k:
                t = jnp.broadcast_to(c[j][k : k + 1, :], (8, n)) * pivot
                c[j] = jnp.where(at_k, t, c[j] - ck * t)
        c[k] = jnp.where(at_k, pivot, -(ck * pivot))
    inside = (lane >= 8 * m) & (lane < 8 * m + 8)
    row = jnp.where(inside, jnp.where(lane - 8 * m == sub, 1.0, 0.0), row)
    new = c[0] * jnp.broadcast_to(row[0:1, :], (8, n))
    for j in range(1, 8):
        new = new + c[j] * jnp.broadcast_to(row[j : j + 1, :], (8, n))
    spread = [jnp.broadcast_to(new[j : j + 1, :], (8, n)) for j in range(8)]
    out = []
    for i, group in enumerate(groups):
        if i == m:
            out.append(new)
            continue
        left = jnp.where(inside, 0.0, group)
        for j in range(8):
            left = left - jnp.broadcast_to(group[:, 8 * m + j : 8 * m + j + 1], (8, n)) * spread[j]
        out.append(left)
    return out


def fdot(a, b):
    return jnp.dot(a, b, precision=HIGHEST, preferred_element_type=F)


def invert128(block, between):
    groups = [block[8 * i : 8 * i + 8, :] for i in range(16)]
    for m in range(16):
        groups = sweep8(groups, m)
        if m % 4 == 3:
            between[m // 4]()
    return jnp.concatenate(groups, axis=0)


def invert_block(x, k, between):
    here = slice(128 * k, 128 * k + 128)
    inverse = invert128(x[here, here], between)
    row = fdot(inverse, x[here, :])
    column = x[:, here]
    x[...] = x[...] - fdot(column, row)
    x[:, here] = -fdot(column, inverse)
    x[here, :] = row
    x[here, here] = inverse


def gather_kernel(h_hbm, w_hbm, p_ref, t_ref, wt_ref, sc_ref, hv, wv, sem):
    row = lax.axis_index("row")
    col = lax.axis_index("col")
    w_copies, h_copies = [], []
    for b in range(3):
        copy = pltpu.make_async_copy(w_hbm.at[:, b, 0, :], wv.at[:, pl.ds(256 * b, 256)], sem.at[18 + b])
        copy.start()
        w_copies.append(copy)
    for a in range(6):
        for b in range(3):
            copy = pltpu.make_async_copy(
                h_hbm.at[a, 0, :, b, 0, :], hv.at[pl.ds(256 * a, 256), pl.ds(256 * b, 256)], sem.at[3 * a + b]
            )
            copy.start()
            h_copies.append(copy)
    cols = local_place(p_ref, 16, col)
    hot = [onehot(cols, 256 * b, 256) for b in range(3)]
    for b in range(3):
        w_copies[b].wait()
        part = dot(split3(wv[:, 256 * b : 256 * b + 256], 1), jnp.concatenate([hot[b]] * 3, axis=1), NT)
        wt_ref[...] = part if b == 0 else wt_ref[...] + part
    rows = local_place(p_ref, 8, row)
    for a in range(6):
        for copy in h_copies[3 * a : 3 * a + 3]:
            copy.wait()
        pick = jnp.concatenate([onehot(rows, 256 * a, 256)] * 3, axis=1)
        part = dot(pick, split3(hv[256 * a : 256 * a + 256, :], 0), NN)
        t_ref[...] = part if a == 0 else t_ref[...] + part
    total = None
    for b in range(3):
        part = dot(split3(t_ref[:, 256 * b : 256 * b + 256], 1), jnp.concatenate([hot[b]] * 3, axis=1), NT)
        total = part if b == 0 else total + part
    for v in range(2):
        for j in range(2):
            lanes = slice(256 * v + 128 * j, 256 * v + 128 * j + 128)
            sc_ref[:, v, :, :, j] = total[:, lanes].reshape(4, 2, 8, 8, 128).transpose(1, 0, 2, 3, 4)


def gather(hinverse, pruned, weights):
    return pl.pallas_call(
        gather_kernel,
        out_shape=[
            jax.ShapeDtypeStruct((512, 768), F),
            jax.ShapeDtypeStruct((768, 512), F),
            jax.ShapeDtypeStruct((2, 2, 4, 8, 2, 8, 128), F),
            jax.ShapeDtypeStruct((1536, 768), F),
            jax.ShapeDtypeStruct((768, 768), F),
        ],
        in_specs=[HBM, HBM, VMEM],
        out_specs=[VMEM] * 5,
        scratch_shapes=[pltpu.SemaphoreType.DMA((21,))],
        compiler_params=pltpu.CompilerParams(vmem_limit_bytes=40 * MIB),
        name="gather",
    )(hinverse, weights, pruned)


def solve_kernel(t, wt, sc, mv, y, w,
                 ra, xbox1, xbox2, wc, wboxf, wboxn, wbox2f, wbox2n,
                 sbox, px, qy, ps, qs, py, qx, sf, pan, ya, xs, send, recv):
    row = lax.axis_index("row")
    col = lax.axis_index("col")
    x, k = row // 2, row % 2
    z, yy = col // 4, col % 4
    cu, cl = col // 2, col % 2

    def dev(r, c):
        return {"row": r, "col": c}

    sibling = dev(2 * x + 1 - k, col)
    x_peers = [dev((row + 2 * d) % 8, col) for d in range(1, 4)]
    peers = [dev(row, (col + d) % 16) for d in range(1, 16)]
    x_up, x_down = x_peers[0], x_peers[2]
    y_up, y_down = dev(row, 4 * z + (yy + 1) % 4), dev(row, 4 * z + (yy + 3) % 4)
    z_up, z_down = peers[3], peers[11]
    target = dev(col % 8, 4 * (2 * (1 - col // 8) + k) + x)
    source = dev(2 * yy + z % 2, row + 8 * (1 - z // 2))

    barrier = pltpu.get_barrier_semaphore()
    greet = [sibling, target, source] + x_peers + peers
    for device in greet:
        pl.semaphore_signal(barrier, inc=1, device_id=device, device_id_type=MESH)
    pl.semaphore_wait(barrier, len(greet))
    links = Links(send, recv)

    first = [links.copy(sc.at[1 - k, v], sbox.at[v], sibling) for v in range(2)]
    order = [(x + 2) % 4, (x + 1) % 4, (x + 3) % 4, x]

    def half_columns(core):
        return pl.ds(pl.multiple_of(384 * core, 128), 384)

    rows_in = [links.copy(t.at[j, :, half_columns(1 - k)], ra.at[j], sibling) for j in order]

    lanes = [pl.ds(0, 256), pl.ds(256, 256)]
    sum_z0 = RingSum(links, z, z_up, z_down, lambda j: wt.at[j, :, :, lanes[0]],
                     (wboxf.at[0], wboxf.at[1], wboxn.at[0], wboxn.at[1]))
    sum_y1 = RingSum(links, yy, y_up, y_down, lambda j: wt.at[:, j, :, lanes[1]],
                     (wboxf.at[2], wboxf.at[3], wboxn.at[2], wboxn.at[3]))
    sum_y0 = RingSum(links, yy, y_up, y_down, lambda j: wc.at[0, j],
                     (wbox2f.at[0], wbox2f.at[1], wbox2n.at[0], wbox2n.at[1]))
    sum_z1 = RingSum(links, z, z_up, z_down, lambda j: wc.at[1, j],
                     (wbox2f.at[2], wbox2f.at[3], wbox2n.at[2], wbox2n.at[3]))
    sum_x = RingSum(links, x, x_up, x_down, lambda j: ra.at[j],
                    (xbox1.at[0], xbox1.at[1], xbox2.at[0], xbox2.at[1]))

    sum_z0.start()
    sum_y1.start()

    first[0].wait_recv()
    sbox[0] = sbox[0] + sc[k, 0]
    p1 = [links.copy(sbox.at[0, (x + d) % 4], px.at[d - 1], x_peers[d - 1]) for d in range(1, 4)]
    first[1].wait_recv()
    sbox[1] = sbox[1] + sc[k, 1]
    q1 = []
    for d in range(1, 16):
        q = (col + d) % 16
        q1.append(links.copy(sbox.at[1, :, q // 2, q % 2], qy.at[d - 1], peers[d - 1]))

    for n, j in enumerate(order):
        rows_in[n].wait_recv()
        ra[j] = ra[j] + t[j, :, half_columns(k)]
    sum_x.start()
    sum_z0.near()
    sum_y1.near()

    total = sbox[0, x]
    for d in range(1, 4):
        p1[d - 1].wait_recv()
        total = total + px[d - 1]
    ps[...] = total
    p2 = []
    for d in range(1, 16):
        q = (col + d) % 16
        p2.append(links.copy(ps.at[q // 2, q % 2], py.at[d - 1], peers[d - 1]))
    sum_x.near()
    total = sbox[1, :, cu, cl]
    for d in range(1, 16):
        q1[d - 1].wait_recv()
        total = total + qy[d - 1]
    qs[...] = total
    q2 = [links.copy(qs.at[(x + d) % 4], qx.at[d - 1], x_peers[d - 1]) for d in range(1, 4)]

    wc[0] = sum_z0.finish()
    wc[1] = sum_y1.finish()
    sum_y0.start()
    sum_z1.start()

    total = ps[cu, cl]
    for d in range(1, 16):
        p2[d - 1].wait_recv()
        total = total + py[d - 1]
    own_p = sf.at[k, 0, x, cu, cl]
    own_p[...] = total
    p3 = [links.copy(own_p, own_p, peers[d - 1]) for d in range(1, 16)]
    total = qs[x]
    for d in range(1, 4):
        q2[d - 1].wait_recv()
        total = total + qx[d - 1]
    own_q = sf.at[k, 1, x, cu, cl]
    own_q[...] = total
    q3 = [links.copy(own_q, own_q, x_peers[d - 1]) for d in range(1, 4)]

    piece = sum_x.finish()
    pan[x, :, half_columns(k)] = piece
    ya[...] = piece.T

    def lane_block(j):
        return pl.ds(pl.multiple_of(128 * j, 128), 128)

    moved = links.copy(ya, y.at[2 * (1 - col // 8) + k, :, lane_block(x)], target)
    sum_y0.near()
    sum_z1.near()

    for copy in q3:
        copy.wait_recv()
    own_q = sf.at[k, 1, :, cu, cl]
    q4 = [links.copy(own_q, own_q, peers[d - 1]) for d in range(1, 16)]
    for copy in p3:
        copy.wait_recv()
    own_p = sf.at[k, 0, x]
    p4 = [links.copy(own_p, own_p, x_peers[d - 1]) for d in range(1, 4)]

    w_y0 = RingGather(links, yy, y_up, y_down, lambda j: w.at[z, j, :, lanes[0]])
    w_z1 = RingGather(links, z, z_up, z_down, lambda j: w.at[j, yy, :, lanes[1]])
    w_z0 = RingGather(links, z, z_up, z_down, lambda j: w.at[j, :, :, lanes[0]])
    w_y1 = RingGather(links, yy, y_up, y_down, lambda j: w.at[:, j, :, lanes[1]])
    upper, lower = pl.ds(0, 192), pl.ds(192, 192)
    y_y0 = RingGather(links, yy, y_up, y_down, lambda j: y.at[z, upper, lane_block(j)])
    y_z1 = RingGather(links, z, z_up, z_down, lambda j: y.at[j, lower, lane_block(yy)])
    y_z0 = RingGather(links, z, z_up, z_down, lambda j: y.at[j, upper])
    y_y1 = RingGather(links, yy, y_up, y_down, lambda j: y.at[:, lower, lane_block(j)])
    pan_x = RingGather(links, x, x_up, x_down, lambda j: pan.at[j, :, half_columns(k)])

    w[z, yy, :, 0:256] = sum_y0.finish()
    w[z, yy, :, 256:512] = sum_z1.finish()
    w_y0.own()
    w_z1.own()

    for copy in q4 + p4:
        copy.wait_recv()
    own_s = sf.at[k]
    swap_s = links.copy(own_s, own_s, sibling)
    pan_x.own()
    w_y0.forward()
    w_z1.forward()
    moved.wait_recv()
    y_y0.own()
    y_z1.own()
    swap_s.wait_recv()
    for v in range(2):
        for j in range(2):
            xs[:, 256 * v + 128 * j : 256 * v + 128 * j + 128] = sf[:, v, :, :, j].transpose(1, 0, 2, 3, 4).reshape(512, 128)

    swaps = []

    def swap_panel():
        pan_x.finish()
        for n in range(4):
            part = pan.at[(x + n) % 4, :, half_columns(k)]
            swaps.append(links.copy(part, part, sibling))

    def steps(*todo):
        def run():
            for step in todo:
                step()

        return run

    places = [
        steps(w_y0.finish, w_z1.finish, w_z0.own, w_y1.own),
        steps(y_y0.forward, y_z1.forward),
        steps(pan_x.forward),
        steps(y_y0.finish, y_z0.own, y_z1.finish, y_y1.own),
        steps(),
        steps(swap_panel, w_z0.forward, w_y1.forward),
        steps(),
        steps(y_z0.forward, y_y1.forward),
    ]
    places += [steps()] * (16 - len(places))
    for n in range(4):
        invert_block(xs, n, places[4 * n : 4 * n + 4])
    for copy in swaps:
        copy.wait_recv()
    ah, al = split2(xs[...])
    bh, bl = split2(pan[...].reshape(512, 768))
    hi, lo = split2(dot(jnp.concatenate([al, ah, ah], axis=1), jnp.concatenate([bh, bl, bh], axis=0), NN))
    mv[0:512, :] = hi
    mv[512:1024, :] = lo
    mv[1024:1536, :] = hi
    w_z0.finish()
    w_y1.finish()
    y_z0.finish()
    y_y1.finish()
    links.drain()


COPIES = 180


def solve(t, wt, sc):
    return pl.pallas_call(
        solve_kernel,
        out_shape=[
            jax.ShapeDtypeStruct((1536, 768), B),
            jax.ShapeDtypeStruct((4, 384, 512), F),
            jax.ShapeDtypeStruct((4, 4, 48, 512), F),
        ],
        in_specs=[VMEM] * 3,
        out_specs=[VMEM] * 3,
        scratch_shapes=[
            pltpu.VMEM((4, 128, 384), F),
            pltpu.VMEM((2, 64, 384), F),
            pltpu.VMEM((2, 128, 384), F),
            pltpu.VMEM((2, 4, 48, 256), F),
            pltpu.VMEM((4, 2, 48, 256), F),
            pltpu.VMEM((4, 4, 48, 256), F),
            pltpu.VMEM((4, 24, 256), F),
            pltpu.VMEM((4, 48, 256), F),
            pltpu.VMEM((2, 4, 8, 2, 8, 128), F),
            pltpu.VMEM((3, 8, 2, 8, 128), F),
            pltpu.VMEM((15, 4, 8, 128), F),
            pltpu.VMEM((8, 2, 8, 128), F),
            pltpu.VMEM((4, 8, 128), F),
            pltpu.VMEM((15, 8, 128), F),
            pltpu.VMEM((3, 8, 128), F),
            pltpu.VMEM((2, 2, 4, 8, 2, 8, 128), F),
            pltpu.VMEM((4, 128, 768), F),
            pltpu.VMEM((384, 128), F),
            pltpu.VMEM((512, 512), F),
            pltpu.SemaphoreType.DMA((COPIES,)),
            pltpu.SemaphoreType.DMA((COPIES,)),
        ],
        compiler_params=pltpu.CompilerParams(vmem_limit_bytes=32 * MIB, collective_id=0, has_side_effects=True),
        name="solve",
    )(t.reshape(4, 128, 768), wt.reshape(4, 4, 48, 512), sc)


def update_kernel(hv, wv, p_ref, mm, yv, wt, ho_hbm, wo_hbm, hn, wn, osem):
    col = lax.axis_index("col")
    cols = local_place(p_ref, 16, col)
    lane = lax.broadcasted_iota(jnp.int32, cols.shape, 1)
    hit = [jnp.max((cols == lane + 128 * q).astype(F), axis=0, keepdims=True) for q in range(6)]
    pruned_here = jnp.concatenate(hit, axis=1) > 0.5
    outs = []

    def put(src, dst):
        copy = pltpu.make_async_copy(src, dst, osem.at[len(outs)])
        copy.start()
        outs.append(copy)

    def product(left):
        hi, lo = split2(left)
        return dot(jnp.concatenate([hi, hi, lo], axis=1), mm[...], NN)

    for block in range(4):
        hi, half = 1 - block // 2, block % 2
        runs = [(2 * (j // 256) + hi, j % 256) for j in (384 * half, 384 * half + 128, 384 * half + 256)]
        change = product(yv[block])
        for u, (a, j) in enumerate(runs):
            here = slice(256 * a + j, 256 * a + j + 128)
            hn[here, :] = hv[here, :] - change[128 * u : 128 * u + 128, :]
            for b in range(3):
                put(hn.at[pl.ds(256 * a + j, 128), pl.ds(256 * b, 256)], ho_hbm.at[a, 0, pl.ds(j, 128), b, 0, :])
    for g in range(2):
        rows = slice(384 * g, 384 * g + 384)
        wn[rows, :] = jnp.where(pruned_here, 0.0, wv[rows, :] - product(wt[rows, :]))
        for b in range(3):
            put(wn.at[pl.ds(384 * g, 384), pl.ds(256 * b, 256)], wo_hbm.at[pl.ds(384 * g, 384), b, 0, :])
    for copy in outs:
        copy.wait()


def update(hinverse, pruned, weights, hv, wv, m, y, wt):
    return pl.pallas_call(
        update_kernel,
        out_shape=[jax.ShapeDtypeStruct(hinverse.shape, F), jax.ShapeDtypeStruct(weights.shape, F)],
        in_specs=[VMEM] * 6,
        out_specs=[HBM, HBM],
        scratch_shapes=[
            pltpu.VMEM((1536, 768), F),
            pltpu.VMEM((768, 768), F),
            pltpu.SemaphoreType.DMA((42,)),
        ],
        compiler_params=pltpu.CompilerParams(vmem_limit_bytes=36 * MIB),
        name="update",
    )(hv, wv, pruned, m, y, wt)


def per_device(hinverse, pruned, weights):
    t, wt, sc, hv, wv = gather(hinverse, pruned, weights)
    m, y, w = solve(t, wt, sc)
    return update(hinverse, pruned, weights, hv, wv, m, y, w.reshape(768, 512))


def solution(mesh):
    placed = (P(None, "row", None, None, "col", None), P(), P("row", None, "col", None))
    return jax.shard_map(
        per_device,
        mesh=mesh,
        in_specs=placed,
        out_specs=(P(None, "row", None, None, "col", None), P("row", None, "col", None)),
        check_vma=False,
    )
```

```python
import jax
import jax.numpy as jnp
from jax import lax
from jax.experimental import pallas as pl
from jax.experimental.pallas import tpu as pltpu
from jax.sharding import PartitionSpec as P

F = jnp.float32
B = jnp.bfloat16
MESH = pl.DeviceIdType.MESH
HIGHEST = lax.Precision.HIGHEST
NN = ((1,), (0,))
NT = ((1,), (1,))
TN = ((0,), (0,))
HBM = pl.BlockSpec(memory_space=pltpu.HBM)
VMEM = pl.BlockSpec(memory_space=pltpu.VMEM)
MIB = 2**20


def split2(x):
    hi = x.astype(B)
    return hi, (x - hi.astype(F)).astype(B)


def parts(x, axis):
    hi, lo = split2(x)
    return jnp.concatenate([lo, hi], axis=axis)


def dot(a, b, dims):
    return lax.dot_general(a, b, (dims, ((), ())), preferred_element_type=F)


def local_place(p_ref, parts, index):
    p = jnp.concatenate([p_ref[0:1, :], p_ref[1:2, :]], axis=1)
    p = jnp.broadcast_to(p, (128, p.shape[1])).T
    tile = p >> 8
    return jnp.where(tile % parts == index, (tile // parts) * 256 + (p & 255), -1)


def onehot(place, start, width):
    lane = lax.broadcasted_iota(jnp.int32, place.shape, 1)
    blocks = [(place == lane + (start + 128 * q)).astype(F).astype(B) for q in range(width // 128)]
    return jnp.concatenate(blocks, axis=1)


class Links:
    def __init__(self, send, recv):
        self.send, self.recv, self.count, self.started = send, recv, 0, []

    def copy(self, src, dst, device):
        n = self.count
        self.count += 1
        made = pltpu.make_async_remote_copy(
            src_ref=src, dst_ref=dst, send_sem=self.send.at[n], recv_sem=self.recv.at[n], device_id=device, device_id_type=MESH
        )
        made.start()
        self.started.append(made)
        return made

    def drain(self):
        for made in self.started:
            made.wait_send()


def halves_of(ref):
    n = ref.shape[0] // 2
    return ref.at[pl.ds(0, n)], ref.at[pl.ds(n, n)]


class RingSum:
    def __init__(self, links, i, up, down, full, boxes):
        self.links, self.i, self.up, self.down, self.full, self.boxes = links, i, up, down, full, boxes

    def start(self):
        left, right, left2, right2 = self.boxes
        far0, far1 = halves_of(self.full((self.i + 2) % 4))
        self.a = self.links.copy(far0, left, self.up)
        self.b = self.links.copy(far1, right, self.down)
        self.c = self.links.copy(halves_of(self.full((self.i + 1) % 4))[1], halves_of(left2)[1], self.up)
        self.d = self.links.copy(halves_of(self.full((self.i + 3) % 4))[0], halves_of(right2)[0], self.down)

    def near(self):
        left, right, left2, right2 = self.boxes
        self.a.wait_recv()
        part = halves_of(self.full((self.i + 1) % 4))[0]
        part[...] = part[...] + left[...]
        self.a = self.links.copy(part, halves_of(left2)[0], self.up)
        self.b.wait_recv()
        part = halves_of(self.full((self.i + 3) % 4))[1]
        part[...] = part[...] + right[...]
        self.b = self.links.copy(part, halves_of(right2)[1], self.down)

    def finish(self):
        _, _, left2, right2 = self.boxes
        for copy in (self.a, self.b, self.c, self.d):
            copy.wait_recv()
        return self.full(self.i)[...] + left2[...] + right2[...]


class RingGather:
    def __init__(self, links, i, up, down, full):
        self.links, self.i, self.up, self.down, self.full = links, i, up, down, full

    def own(self):
        first, second = halves_of(self.full(self.i))
        self.a = self.links.copy(first, first, self.up)
        self.b = self.links.copy(second, second, self.down)
        self.c = self.links.copy(second, second, self.up)
        self.d = self.links.copy(first, first, self.down)

    def forward(self):
        self.a.wait_recv()
        part = halves_of(self.full((self.i + 3) % 4))[0]
        self.a = self.links.copy(part, part, self.up)
        self.b.wait_recv()
        part = halves_of(self.full((self.i + 1) % 4))[1]
        self.b = self.links.copy(part, part, self.down)

    def finish(self):
        for copy in (self.a, self.b, self.c, self.d):
            copy.wait_recv()


def sweep8(groups, m):
    n = 8 * len(groups)
    row = groups[m]
    sub = lax.broadcasted_iota(jnp.int32, (8, n), 0)
    lane = lax.broadcasted_iota(jnp.int32, (8, n), 1)
    c = [jnp.broadcast_to(row[:, 8 * m + j : 8 * m + j + 1], (8, n)) for j in range(8)]
    for k in range(8):
        pivot = 1.0 / jnp.broadcast_to(c[k][k : k + 1, :], (8, n))
        at_k = sub == k
        ck = c[k]
        for j in range(8):
            if j != k:
                t = jnp.broadcast_to(c[j][k : k + 1, :], (8, n)) * pivot
                c[j] = jnp.where(at_k, t, c[j] - ck * t)
        c[k] = jnp.where(at_k, pivot, -(ck * pivot))
    inside = (lane >= 8 * m) & (lane < 8 * m + 8)
    row = jnp.where(inside, jnp.where(lane - 8 * m == sub, 1.0, 0.0), row)
    new = c[0] * jnp.broadcast_to(row[0:1, :], (8, n))
    for j in range(1, 8):
        new = new + c[j] * jnp.broadcast_to(row[j : j + 1, :], (8, n))
    spread = [jnp.broadcast_to(new[j : j + 1, :], (8, n)) for j in range(8)]
    out = []
    for i, group in enumerate(groups):
        if i == m:
            out.append(new)
            continue
        left = jnp.where(inside, 0.0, group)
        for j in range(8):
            left = left - jnp.broadcast_to(group[:, 8 * m + j : 8 * m + j + 1], (8, n)) * spread[j]
        out.append(left)
    return out


def fdot(a, b):
    return jnp.dot(a, b, precision=HIGHEST, preferred_element_type=F)


def invert128(block, between):
    groups = [block[8 * i : 8 * i + 8, :] for i in range(16)]
    for m in range(16):
        groups = sweep8(groups, m)
        if m % 4 == 3:
            between[m // 4]()
    return jnp.concatenate(groups, axis=0)


def invert_block(x, k, between):
    here = slice(128 * k, 128 * k + 128)
    inverse = invert128(x[here, here], between)
    row = fdot(inverse, x[here, :])
    column = x[:, here]
    x[...] = x[...] - fdot(column, row)
    x[:, here] = -fdot(column, inverse)
    x[here, :] = row
    x[here, here] = inverse


def load(h_hbm, w_hbm, hv, wv, sem):
    w_copies, h_copies = [], []
    for b in range(3):
        copy = pltpu.make_async_copy(w_hbm.at[:, b, 0, :], wv.at[:, pl.ds(256 * b, 256)], sem.at[18 + b])
        copy.start()
        w_copies.append(copy)
    for a in range(6):
        for b in range(3):
            copy = pltpu.make_async_copy(
                h_hbm.at[a, 0, :, b, 0, :], hv.at[pl.ds(256 * a, 256), pl.ds(256 * b, 256)], sem.at[3 * a + b]
            )
            copy.start()
            h_copies.append(copy)
    return h_copies, w_copies


def gather_kernel(h_hbm, w_hbm, p_ref, t_ref, wt_ref, sc_ref, hv, wv, sem):
    row = lax.axis_index("row")
    col = lax.axis_index("col")
    h_copies, w_copies = load(h_hbm, w_hbm, hv, wv, sem)
    cols = local_place(p_ref, 16, col)
    hot = [onehot(cols, 256 * b, 256) for b in range(3)]
    for b in range(3):
        w_copies[b].wait()
        part = dot(parts(wv[:, 256 * b : 256 * b + 256], 1), jnp.concatenate([hot[b]] * 2, axis=1), NT)
        wt_ref[...] = part if b == 0 else wt_ref[...] + part
    rows = local_place(p_ref, 8, row)
    for a in range(6):
        for copy in h_copies[3 * a : 3 * a + 3]:
            copy.wait()
        pick = jnp.concatenate([onehot(rows, 256 * a, 256)] * 2, axis=1)
        part = dot(pick, parts(hv[256 * a : 256 * a + 256, :], 0), NN)
        t_ref[...] = part if a == 0 else t_ref[...] + part
    total = None
    for b in range(3):
        part = dot(parts(t_ref[:, 256 * b : 256 * b + 256], 1), jnp.concatenate([hot[b]] * 2, axis=1), NT)
        total = part if b == 0 else total + part
    for v in range(2):
        for j in range(2):
            lanes = slice(256 * v + 128 * j, 256 * v + 128 * j + 128)
            sc_ref[:, v, :, :, j] = total[:, lanes].reshape(4, 2, 8, 8, 128).transpose(1, 0, 2, 3, 4)


def gather(hinverse, pruned, weights):
    return pl.pallas_call(
        gather_kernel,
        out_shape=[
            jax.ShapeDtypeStruct((512, 768), F),
            jax.ShapeDtypeStruct((768, 512), F),
            jax.ShapeDtypeStruct((2, 2, 4, 8, 2, 8, 128), F),
        ],
        in_specs=[HBM, HBM, VMEM],
        out_specs=[VMEM] * 3,
        scratch_shapes=[
            pltpu.VMEM((1536, 768), F),
            pltpu.VMEM((768, 768), F),
            pltpu.SemaphoreType.DMA((21,)),
        ],
        compiler_params=pltpu.CompilerParams(vmem_limit_bytes=48 * MIB),
        name="gather",
    )(hinverse, weights, pruned)


def solve_kernel(t, wt, sc, h_hbm, w_hbm, mv, y, w, hv, wv,
                 ra, xbox1, xbox2, wc, wboxf, wboxn, wbox2f, wbox2n,
                 sbox, px, qy, ps, qs, py, qx, sf, pan, ya, xs, send, recv, sem):
    row = lax.axis_index("row")
    col = lax.axis_index("col")
    x, k = row // 2, row % 2
    z, yy = col // 4, col % 4
    cu, cl = col // 2, col % 2

    def dev(r, c):
        return {"row": r, "col": c}

    sibling = dev(2 * x + 1 - k, col)
    x_peers = [dev((row + 2 * d) % 8, col) for d in range(1, 4)]
    peers = [dev(row, (col + d) % 16) for d in range(1, 16)]
    x_up, x_down = x_peers[0], x_peers[2]
    y_up, y_down = dev(row, 4 * z + (yy + 1) % 4), dev(row, 4 * z + (yy + 3) % 4)
    z_up, z_down = peers[3], peers[11]
    target = dev(col % 8, 4 * (2 * (1 - col // 8) + k) + x)
    source = dev(2 * yy + z % 2, row + 8 * (1 - z // 2))

    h_copies, w_copies = load(h_hbm, w_hbm, hv, wv, sem)
    barrier = pltpu.get_barrier_semaphore()
    greet = [sibling, target, source] + x_peers + peers
    for device in greet:
        pl.semaphore_signal(barrier, inc=1, device_id=device, device_id_type=MESH)
    pl.semaphore_wait(barrier, len(greet))
    links = Links(send, recv)

    first = [links.copy(sc.at[1 - k, v], sbox.at[v], sibling) for v in range(2)]
    order = [(x + 2) % 4, (x + 1) % 4, (x + 3) % 4, x]

    def half_columns(core):
        return pl.ds(pl.multiple_of(384 * core, 128), 384)

    rows_in = [links.copy(t.at[j, :, half_columns(1 - k)], ra.at[j], sibling) for j in order]

    lanes = [pl.ds(0, 256), pl.ds(256, 256)]
    sum_z0 = RingSum(links, z, z_up, z_down, lambda j: wt.at[j, :, :, lanes[0]],
                     (wboxf.at[0], wboxf.at[1], wboxn.at[0], wboxn.at[1]))
    sum_y1 = RingSum(links, yy, y_up, y_down, lambda j: wt.at[:, j, :, lanes[1]],
                     (wboxf.at[2], wboxf.at[3], wboxn.at[2], wboxn.at[3]))
    sum_y0 = RingSum(links, yy, y_up, y_down, lambda j: wc.at[0, j],
                     (wbox2f.at[0], wbox2f.at[1], wbox2n.at[0], wbox2n.at[1]))
    sum_z1 = RingSum(links, z, z_up, z_down, lambda j: wc.at[1, j],
                     (wbox2f.at[2], wbox2f.at[3], wbox2n.at[2], wbox2n.at[3]))
    sum_x = RingSum(links, x, x_up, x_down, lambda j: ra.at[j],
                    (xbox1.at[0], xbox1.at[1], xbox2.at[0], xbox2.at[1]))

    first[0].wait_recv()
    sbox[0] = sbox[0] + sc[k, 0]
    p1 = [links.copy(sbox.at[0, (x + d) % 4], px.at[d - 1], x_peers[d - 1]) for d in range(1, 4)]
    first[1].wait_recv()
    sbox[1] = sbox[1] + sc[k, 1]
    q1 = []
    for d in range(1, 16):
        q = (col + d) % 16
        q1.append(links.copy(sbox.at[1, :, q // 2, q % 2], qy.at[d - 1], peers[d - 1]))

    sum_z0.start()
    sum_y1.start()
    for n, j in enumerate(order):
        rows_in[n].wait_recv()
        ra[j] = ra[j] + t[j, :, half_columns(k)]
    sum_x.start()

    total = sbox[0, x]
    for d in range(1, 4):
        p1[d - 1].wait_recv()
        total = total + px[d - 1]
    ps[...] = total
    p2 = []
    for d in range(1, 16):
        q = (col + d) % 16
        p2.append(links.copy(ps.at[q // 2, q % 2], py.at[d - 1], peers[d - 1]))
    total = sbox[1, :, cu, cl]
    for d in range(1, 16):
        q1[d - 1].wait_recv()
        total = total + qy[d - 1]
    qs[...] = total
    q2 = [links.copy(qs.at[(x + d) % 4], qx.at[d - 1], x_peers[d - 1]) for d in range(1, 4)]

    sum_x.near()
    sum_z0.near()
    sum_y1.near()

    total = ps[cu, cl]
    for d in range(1, 16):
        p2[d - 1].wait_recv()
        total = total + py[d - 1]
    own_p = sf.at[k, 0, x, cu, cl]
    own_p[...] = total
    p3 = [links.copy(own_p, own_p, peers[d - 1]) for d in range(1, 16)]
    total = qs[x]
    for d in range(1, 4):
        q2[d - 1].wait_recv()
        total = total + qx[d - 1]
    own_q = sf.at[k, 1, x, cu, cl]
    own_q[...] = total
    q3 = [links.copy(own_q, own_q, x_peers[d - 1]) for d in range(1, 4)]

    for copy in q3:
        copy.wait_recv()
    own_q = sf.at[k, 1, :, cu, cl]
    q4 = [links.copy(own_q, own_q, peers[d - 1]) for d in range(1, 16)]
    for copy in p3:
        copy.wait_recv()
    own_p = sf.at[k, 0, x]
    p4 = [links.copy(own_p, own_p, x_peers[d - 1]) for d in range(1, 4)]

    piece = sum_x.finish()
    pan[x, :, half_columns(k)] = piece
    ya[...] = piece.T

    def lane_block(j):
        return pl.ds(pl.multiple_of(128 * j, 128), 128)

    moved = links.copy(ya, y.at[2 * (1 - col // 8) + k, :, lane_block(x)], target)

    w_y0 = RingGather(links, yy, y_up, y_down, lambda j: w.at[z, j, :, lanes[0]])
    w_z1 = RingGather(links, z, z_up, z_down, lambda j: w.at[j, yy, :, lanes[1]])
    w_z0 = RingGather(links, z, z_up, z_down, lambda j: w.at[j, :, :, lanes[0]])
    w_y1 = RingGather(links, yy, y_up, y_down, lambda j: w.at[:, j, :, lanes[1]])
    upper, lower = pl.ds(0, 192), pl.ds(192, 192)
    y_y0 = RingGather(links, yy, y_up, y_down, lambda j: y.at[z, upper, lane_block(j)])
    y_z1 = RingGather(links, z, z_up, z_down, lambda j: y.at[j, lower, lane_block(yy)])
    y_z0 = RingGather(links, z, z_up, z_down, lambda j: y.at[j, upper])
    y_y1 = RingGather(links, yy, y_up, y_down, lambda j: y.at[:, lower, lane_block(j)])
    pan_x = RingGather(links, x, x_up, x_down, lambda j: pan.at[j, :, half_columns(k)])

    wc[0] = sum_z0.finish()
    wc[1] = sum_y1.finish()
    sum_y0.start()
    sum_z1.start()

    for copy in q4 + p4:
        copy.wait_recv()
    own_s = sf.at[k]
    swap_s = links.copy(own_s, own_s, sibling)
    pan_x.own()
    sum_y0.near()
    sum_z1.near()
    swap_s.wait_recv()
    for v in range(2):
        for j in range(2):
            xs[:, 256 * v + 128 * j : 256 * v + 128 * j + 128] = sf[:, v, :, :, j].transpose(1, 0, 2, 3, 4).reshape(512, 128)

    swaps = []

    def start_columns():
        moved.wait_recv()
        y_y0.own()
        y_z1.own()

    def start_weights():
        w[z, yy, :, 0:256] = sum_y0.finish()
        w[z, yy, :, 256:512] = sum_z1.finish()
        w_y0.own()
        w_z1.own()

    def swap_panel():
        pan_x.finish()
        for n in range(4):
            part = pan.at[(x + n) % 4, :, half_columns(k)]
            swaps.append(links.copy(part, part, sibling))

    def steps(*todo):
        def run():
            for step in todo:
                step()

        return run

    places = [
        steps(start_columns),
        steps(start_weights),
        steps(y_y0.forward, y_z1.forward, pan_x.forward),
        steps(w_y0.forward, w_z1.forward),
        steps(y_y0.finish, y_z0.own, y_z1.finish, y_y1.own),
        steps(w_y0.finish, w_z1.finish, w_z0.own, w_y1.own),
        steps(swap_panel),
        steps(),
        steps(y_z0.forward, y_y1.forward),
        steps(),
        steps(w_z0.forward, w_y1.forward),
    ]
    places += [steps()] * (16 - len(places))
    for n in range(4):
        invert_block(xs, n, places[4 * n : 4 * n + 4])
    for copy in swaps:
        copy.wait_recv()
    ah, al = split2(xs[...])
    bh, bl = split2(pan[...].reshape(512, 768))
    hi, lo = split2(dot(jnp.concatenate([al, ah, ah], axis=1), jnp.concatenate([bh, bl, bh], axis=0), NN))
    mv[0:512, :] = hi
    mv[512:1024, :] = lo
    mv[1024:1536, :] = hi
    w_z0.finish()
    w_y1.finish()
    y_z0.finish()
    y_y1.finish()
    for copy in h_copies + w_copies:
        copy.wait()
    links.drain()


COPIES = 180


def solve(t, wt, sc, hinverse, weights):
    return pl.pallas_call(
        solve_kernel,
        out_shape=[
            jax.ShapeDtypeStruct((1536, 768), B),
            jax.ShapeDtypeStruct((4, 384, 512), F),
            jax.ShapeDtypeStruct((4, 4, 48, 512), F),
            jax.ShapeDtypeStruct((1536, 768), F),
            jax.ShapeDtypeStruct((768, 768), F),
        ],
        in_specs=[VMEM] * 3 + [HBM] * 2,
        out_specs=[VMEM] * 5,
        scratch_shapes=[
            pltpu.VMEM((4, 128, 384), F),
            pltpu.VMEM((2, 64, 384), F),
            pltpu.VMEM((2, 128, 384), F),
            pltpu.VMEM((2, 4, 48, 256), F),
            pltpu.VMEM((4, 2, 48, 256), F),
            pltpu.VMEM((4, 4, 48, 256), F),
            pltpu.VMEM((4, 24, 256), F),
            pltpu.VMEM((4, 48, 256), F),
            pltpu.VMEM((2, 4, 8, 2, 8, 128), F),
            pltpu.VMEM((3, 8, 2, 8, 128), F),
            pltpu.VMEM((15, 4, 8, 128), F),
            pltpu.VMEM((8, 2, 8, 128), F),
            pltpu.VMEM((4, 8, 128), F),
            pltpu.VMEM((15, 8, 128), F),
            pltpu.VMEM((3, 8, 128), F),
            pltpu.VMEM((2, 2, 4, 8, 2, 8, 128), F),
            pltpu.VMEM((4, 128, 768), F),
            pltpu.VMEM((384, 128), F),
            pltpu.VMEM((512, 512), F),
            pltpu.SemaphoreType.DMA((COPIES,)),
            pltpu.SemaphoreType.DMA((COPIES,)),
            pltpu.SemaphoreType.DMA((21,)),
        ],
        compiler_params=pltpu.CompilerParams(vmem_limit_bytes=32 * MIB, collective_id=0, has_side_effects=True),
        name="solve",
    )(t.reshape(4, 128, 768), wt.reshape(4, 4, 48, 512), sc, hinverse, weights)


def update_kernel(hv, wv, p_ref, mm, yv, wt, ho_hbm, wo_hbm, hn, wn, osem):
    col = lax.axis_index("col")
    cols = local_place(p_ref, 16, col)
    lane = lax.broadcasted_iota(jnp.int32, cols.shape, 1)
    hit = [jnp.max((cols == lane + 128 * q).astype(F), axis=0, keepdims=True) for q in range(6)]
    pruned_here = jnp.concatenate(hit, axis=1) > 0.5
    outs = []

    def put(src, dst):
        copy = pltpu.make_async_copy(src, dst, osem.at[len(outs)])
        copy.start()
        outs.append(copy)

    def product(left):
        hi, lo = split2(left)
        return dot(jnp.concatenate([hi, hi, lo], axis=1), mm[...], NN)

    for hi in range(2):
        change = product(yv[2 - 2 * hi : 4 - 2 * hi].reshape(768, 512))
        for n in range(3):
            a = 2 * n + hi
            here = slice(256 * a, 256 * a + 256)
            hn[here, :] = hv[here, :] - change[256 * n : 256 * n + 256, :]
            for b in range(3):
                put(hn.at[pl.ds(256 * a, 256), pl.ds(256 * b, 256)], ho_hbm.at[a, 0, :, b, 0, :])
    wn[...] = jnp.where(pruned_here, 0.0, wv[...] - product(wt[...]))
    for b in range(3):
        put(wn.at[:, pl.ds(256 * b, 256)], wo_hbm.at[:, b, 0, :])
    for copy in outs:
        copy.wait()


def update(hinverse, pruned, weights, hv, wv, m, y, wt):
    return pl.pallas_call(
        update_kernel,
        out_shape=[jax.ShapeDtypeStruct(hinverse.shape, F), jax.ShapeDtypeStruct(weights.shape, F)],
        in_specs=[VMEM] * 6,
        out_specs=[HBM, HBM],
        scratch_shapes=[
            pltpu.VMEM((1536, 768), F),
            pltpu.VMEM((768, 768), F),
            pltpu.SemaphoreType.DMA((21,)),
        ],
        compiler_params=pltpu.CompilerParams(vmem_limit_bytes=36 * MIB),
        name="update",
    )(hv, wv, pruned, m, y, wt)


def per_device(hinverse, pruned, weights):
    t, wt, sc = gather(hinverse, pruned, weights)
    m, y, w, hv, wv = solve(t, wt, sc, hinverse, weights)
    return update(hinverse, pruned, weights, hv, wv, m, y, w.reshape(768, 512))


def solution(mesh):
    placed = (P(None, "row", None, None, "col", None), P(), P("row", None, "col", None))
    return jax.shard_map(
        per_device,
        mesh=mesh,
        in_specs=placed,
        out_specs=(P(None, "row", None, None, "col", None), P("row", None, "col", None)),
        check_vma=False,
    )
```

```python
import jax
import jax.numpy as jnp
from jax import lax
from jax.experimental import pallas as pl
from jax.experimental.pallas import tpu as pltpu
from jax.sharding import PartitionSpec as P

F = jnp.float32
B = jnp.bfloat16
MESH = pl.DeviceIdType.MESH
HIGHEST = lax.Precision.HIGHEST
NN = ((1,), (0,))
NT = ((1,), (1,))
TN = ((0,), (0,))
HBM = pl.BlockSpec(memory_space=pltpu.HBM)
VMEM = pl.BlockSpec(memory_space=pltpu.VMEM)
MIB = 2**20


def split2(x):
    hi = x.astype(B)
    return hi, (x - hi.astype(F)).astype(B)


def parts(x, axis):
    hi, lo = split2(x)
    return jnp.concatenate([lo, hi], axis=axis)


def dot(a, b, dims):
    return lax.dot_general(a, b, (dims, ((), ())), preferred_element_type=F)


def local_place(p_ref, parts, index):
    p = jnp.concatenate([p_ref[0:1, :], p_ref[1:2, :]], axis=1)
    p = jnp.broadcast_to(p, (128, p.shape[1])).T
    tile = p >> 8
    return jnp.where(tile % parts == index, (tile // parts) * 256 + (p & 255), -1)


def onehot(place, start, width):
    lane = lax.broadcasted_iota(jnp.int32, place.shape, 1)
    blocks = [(place == lane + (start + 128 * q)).astype(F).astype(B) for q in range(width // 128)]
    return jnp.concatenate(blocks, axis=1)


class Links:
    def __init__(self, send, recv):
        self.send, self.recv, self.count, self.started = send, recv, 0, []

    def copy(self, src, dst, device):
        n = self.count
        self.count += 1
        made = pltpu.make_async_remote_copy(
            src_ref=src, dst_ref=dst, send_sem=self.send.at[n], recv_sem=self.recv.at[n], device_id=device, device_id_type=MESH
        )
        made.start()
        self.started.append(made)
        return made

    def drain(self):
        for made in self.started:
            made.wait_send()


def halves_of(ref):
    n = ref.shape[0] // 2
    return ref.at[pl.ds(0, n)], ref.at[pl.ds(n, n)]


class RingSum:
    def __init__(self, links, i, up, down, full, boxes):
        self.links, self.i, self.up, self.down, self.full, self.boxes = links, i, up, down, full, boxes

    def start(self):
        left, right, left2, right2 = self.boxes
        far0, far1 = halves_of(self.full((self.i + 2) % 4))
        self.a = self.links.copy(far0, left, self.up)
        self.b = self.links.copy(far1, right, self.down)
        self.c = self.links.copy(halves_of(self.full((self.i + 1) % 4))[1], halves_of(left2)[1], self.up)
        self.d = self.links.copy(halves_of(self.full((self.i + 3) % 4))[0], halves_of(right2)[0], self.down)

    def near(self):
        left, right, left2, right2 = self.boxes
        self.a.wait_recv()
        part = halves_of(self.full((self.i + 1) % 4))[0]
        part[...] = part[...] + left[...]
        self.a = self.links.copy(part, halves_of(left2)[0], self.up)
        self.b.wait_recv()
        part = halves_of(self.full((self.i + 3) % 4))[1]
        part[...] = part[...] + right[...]
        self.b = self.links.copy(part, halves_of(right2)[1], self.down)

    def finish(self):
        _, _, left2, right2 = self.boxes
        for copy in (self.a, self.b, self.c, self.d):
            copy.wait_recv()
        return self.full(self.i)[...] + left2[...] + right2[...]


class RingGather:
    def __init__(self, links, i, up, down, full):
        self.links, self.i, self.up, self.down, self.full = links, i, up, down, full

    def own(self):
        first, second = halves_of(self.full(self.i))
        self.a = self.links.copy(first, first, self.up)
        self.b = self.links.copy(second, second, self.down)
        self.c = self.links.copy(second, second, self.up)
        self.d = self.links.copy(first, first, self.down)

    def forward(self):
        self.a.wait_recv()
        part = halves_of(self.full((self.i + 3) % 4))[0]
        self.a = self.links.copy(part, part, self.up)
        self.b.wait_recv()
        part = halves_of(self.full((self.i + 1) % 4))[1]
        self.b = self.links.copy(part, part, self.down)

    def finish(self):
        for copy in (self.a, self.b, self.c, self.d):
            copy.wait_recv()


def sweep8(groups, m):
    n = 8 * len(groups)
    row = groups[m]
    sub = lax.broadcasted_iota(jnp.int32, (8, n), 0)
    lane = lax.broadcasted_iota(jnp.int32, (8, n), 1)
    c = [jnp.broadcast_to(row[:, 8 * m + j : 8 * m + j + 1], (8, n)) for j in range(8)]
    for k in range(8):
        pivot = 1.0 / jnp.broadcast_to(c[k][k : k + 1, :], (8, n))
        at_k = sub == k
        ck = c[k]
        for j in range(8):
            if j != k:
                t = jnp.broadcast_to(c[j][k : k + 1, :], (8, n)) * pivot
                c[j] = jnp.where(at_k, t, c[j] - ck * t)
        c[k] = jnp.where(at_k, pivot, -(ck * pivot))
    inside = (lane >= 8 * m) & (lane < 8 * m + 8)
    row = jnp.where(inside, jnp.where(lane - 8 * m == sub, 1.0, 0.0), row)
    new = c[0] * jnp.broadcast_to(row[0:1, :], (8, n))
    for j in range(1, 8):
        new = new + c[j] * jnp.broadcast_to(row[j : j + 1, :], (8, n))
    spread = [jnp.broadcast_to(new[j : j + 1, :], (8, n)) for j in range(8)]
    out = []
    for i, group in enumerate(groups):
        if i == m:
            out.append(new)
            continue
        left = jnp.where(inside, 0.0, group)
        for j in range(8):
            left = left - jnp.broadcast_to(group[:, 8 * m + j : 8 * m + j + 1], (8, n)) * spread[j]
        out.append(left)
    return out


def fdot(a, b):
    return jnp.dot(a, b, precision=HIGHEST, preferred_element_type=F)


def invert128(block, between):
    groups = [block[8 * i : 8 * i + 8, :] for i in range(16)]
    for m in range(16):
        groups = sweep8(groups, m)
        if m % 4 == 3:
            between[m // 4]()
    return jnp.concatenate(groups, axis=0)


def invert_block(x, k, between):
    here = slice(128 * k, 128 * k + 128)
    inverse = invert128(x[here, here], between)
    row = fdot(inverse, x[here, :])
    column = x[:, here]
    x[...] = x[...] - fdot(column, row)
    x[:, here] = -fdot(column, inverse)
    x[here, :] = row
    x[here, here] = inverse


def load(h_hbm, w_hbm, hv, wv, sem):
    w_copies, h_copies = [], []
    for b in range(3):
        copy = pltpu.make_async_copy(w_hbm.at[:, b, 0, :], wv.at[:, pl.ds(256 * b, 256)], sem.at[18 + b])
        copy.start()
        w_copies.append(copy)
    for a in range(6):
        for b in range(3):
            copy = pltpu.make_async_copy(
                h_hbm.at[a, 0, :, b, 0, :], hv.at[pl.ds(256 * a, 256), pl.ds(256 * b, 256)], sem.at[3 * a + b]
            )
            copy.start()
            h_copies.append(copy)
    return h_copies, w_copies


def gather_kernel(h_hbm, w_hbm, p_ref, t_ref, wt_ref, sc_ref, hv, wv, sem):
    row = lax.axis_index("row")
    col = lax.axis_index("col")
    h_copies, w_copies = load(h_hbm, w_hbm, hv, wv, sem)
    cols = local_place(p_ref, 16, col)
    hot = [onehot(cols, 256 * b, 256) for b in range(3)]
    for b in range(3):
        w_copies[b].wait()
        part = dot(parts(wv[:, 256 * b : 256 * b + 256], 1), jnp.concatenate([hot[b]] * 2, axis=1), NT)
        wt_ref[...] = part if b == 0 else wt_ref[...] + part
    rows = local_place(p_ref, 8, row)
    for a in range(6):
        for copy in h_copies[3 * a : 3 * a + 3]:
            copy.wait()
        pick = jnp.concatenate([onehot(rows, 256 * a, 256)] * 2, axis=1)
        part = dot(pick, parts(hv[256 * a : 256 * a + 256, :], 0), NN)
        t_ref[...] = part if a == 0 else t_ref[...] + part
    total = None
    for b in range(3):
        part = dot(parts(t_ref[:, 256 * b : 256 * b + 256], 1), jnp.concatenate([hot[b]] * 2, axis=1), NT)
        total = part if b == 0 else total + part
    for v in range(2):
        for j in range(2):
            lanes = slice(256 * v + 128 * j, 256 * v + 128 * j + 128)
            sc_ref[:, v, :, :, j] = total[:, lanes].reshape(4, 2, 8, 8, 128).transpose(1, 0, 2, 3, 4)


def gather(hinverse, pruned, weights):
    return pl.pallas_call(
        gather_kernel,
        out_shape=[
            jax.ShapeDtypeStruct((512, 768), F),
            jax.ShapeDtypeStruct((768, 512), F),
            jax.ShapeDtypeStruct((2, 2, 4, 8, 2, 8, 128), F),
        ],
        in_specs=[HBM, HBM, VMEM],
        out_specs=[VMEM] * 3,
        scratch_shapes=[
            pltpu.VMEM((1536, 768), F),
            pltpu.VMEM((768, 768), F),
            pltpu.SemaphoreType.DMA((21,)),
        ],
        compiler_params=pltpu.CompilerParams(vmem_limit_bytes=48 * MIB),
        name="gather",
    )(hinverse, weights, pruned)


def solve_kernel(t, wt, sc, h_hbm, w_hbm, mv, y, w, hv, wv,
                 ra, xbox1, xbox2, wc, wboxf, wboxn, wbox2f, wbox2n,
                 sbox, px, qy, ps, qs, py, qx, sf, pan, ya, xs, send, recv, sem):
    row = lax.axis_index("row")
    col = lax.axis_index("col")
    x, k = row // 2, row % 2
    z, yy = col // 4, col % 4
    cu, cl = col // 2, col % 2

    def dev(r, c):
        return {"row": r, "col": c}

    sibling = dev(2 * x + 1 - k, col)
    x_peers = [dev((row + 2 * d) % 8, col) for d in range(1, 4)]
    peers = [dev(row, (col + d) % 16) for d in range(1, 16)]
    x_up, x_down = x_peers[0], x_peers[2]
    y_up, y_down = dev(row, 4 * z + (yy + 1) % 4), dev(row, 4 * z + (yy + 3) % 4)
    z_up, z_down = peers[3], peers[11]
    target = dev(col % 8, 4 * (2 * (1 - col // 8) + k) + x)
    source = dev(2 * yy + z % 2, row + 8 * (1 - z // 2))

    h_copies, w_copies = load(h_hbm, w_hbm, hv, wv, sem)
    barrier = pltpu.get_barrier_semaphore()
    greet = [sibling, target, source] + x_peers + peers
    for device in greet:
        pl.semaphore_signal(barrier, inc=1, device_id=device, device_id_type=MESH)
    pl.semaphore_wait(barrier, len(greet))
    links = Links(send, recv)

    first = [links.copy(sc.at[1 - k, v], sbox.at[v], sibling) for v in range(2)]
    order = [(x + 2) % 4, (x + 1) % 4, (x + 3) % 4, x]

    def half_columns(core):
        return pl.ds(pl.multiple_of(384 * core, 128), 384)

    rows_in = [links.copy(t.at[j, :, half_columns(1 - k)], ra.at[j], sibling) for j in order]

    lanes = [pl.ds(0, 256), pl.ds(256, 256)]
    sum_z0 = RingSum(links, z, z_up, z_down, lambda j: wt.at[j, :, :, lanes[0]],
                     (wboxf.at[0], wboxf.at[1], wboxn.at[0], wboxn.at[1]))
    sum_y1 = RingSum(links, yy, y_up, y_down, lambda j: wt.at[:, j, :, lanes[1]],
                     (wboxf.at[2], wboxf.at[3], wboxn.at[2], wboxn.at[3]))
    sum_y0 = RingSum(links, yy, y_up, y_down, lambda j: wc.at[0, j],
                     (wbox2f.at[0], wbox2f.at[1], wbox2n.at[0], wbox2n.at[1]))
    sum_z1 = RingSum(links, z, z_up, z_down, lambda j: wc.at[1, j],
                     (wbox2f.at[2], wbox2f.at[3], wbox2n.at[2], wbox2n.at[3]))
    sum_x = RingSum(links, x, x_up, x_down, lambda j: ra.at[j],
                    (xbox1.at[0], xbox1.at[1], xbox2.at[0], xbox2.at[1]))

    first[0].wait_recv()
    sbox[0] = sbox[0] + sc[k, 0]
    p1 = [links.copy(sbox.at[0, (x + d) % 4], px.at[d - 1], x_peers[d - 1]) for d in range(1, 4)]
    first[1].wait_recv()
    sbox[1] = sbox[1] + sc[k, 1]
    q1 = []
    for d in range(1, 16):
        q = (col + d) % 16
        q1.append(links.copy(sbox.at[1, :, q // 2, q % 2], qy.at[d - 1], peers[d - 1]))

    sum_z0.start()
    sum_y1.start()
    for n, j in enumerate(order):
        rows_in[n].wait_recv()
        ra[j] = ra[j] + t[j, :, half_columns(k)]
    sum_x.start()

    total = sbox[0, x]
    for d in range(1, 4):
        p1[d - 1].wait_recv()
        total = total + px[d - 1]
    ps[...] = total
    p2 = []
    for d in range(1, 16):
        q = (col + d) % 16
        p2.append(links.copy(ps.at[q // 2, q % 2], py.at[d - 1], peers[d - 1]))
    total = sbox[1, :, cu, cl]
    for d in range(1, 16):
        q1[d - 1].wait_recv()
        total = total + qy[d - 1]
    qs[...] = total
    q2 = [links.copy(qs.at[(x + d) % 4], qx.at[d - 1], x_peers[d - 1]) for d in range(1, 4)]

    sum_x.near()
    sum_z0.near()
    sum_y1.near()

    total = ps[cu, cl]
    for d in range(1, 16):
        p2[d - 1].wait_recv()
        total = total + py[d - 1]
    own_p = sf.at[k, 0, x, cu, cl]
    own_p[...] = total
    p3 = [links.copy(own_p, own_p, peers[d - 1]) for d in range(1, 16)]
    total = qs[x]
    for d in range(1, 4):
        q2[d - 1].wait_recv()
        total = total + qx[d - 1]
    own_q = sf.at[k, 1, x, cu, cl]
    own_q[...] = total
    q3 = [links.copy(own_q, own_q, x_peers[d - 1]) for d in range(1, 4)]

    for copy in q3:
        copy.wait_recv()
    own_q = sf.at[k, 1, :, cu, cl]
    q4 = [links.copy(own_q, own_q, peers[d - 1]) for d in range(1, 16)]
    for copy in p3:
        copy.wait_recv()
    own_p = sf.at[k, 0, x]
    p4 = [links.copy(own_p, own_p, x_peers[d - 1]) for d in range(1, 4)]

    piece = sum_x.finish()
    pan[x, :, half_columns(k)] = piece
    ya[...] = piece.T

    def lane_block(j):
        return pl.ds(pl.multiple_of(128 * j, 128), 128)

    moved = links.copy(ya, y.at[2 * (1 - col // 8) + k, :, lane_block(x)], target)

    w_y0 = RingGather(links, yy, y_up, y_down, lambda j: w.at[z, j, :, lanes[0]])
    w_z1 = RingGather(links, z, z_up, z_down, lambda j: w.at[j, yy, :, lanes[1]])
    w_z0 = RingGather(links, z, z_up, z_down, lambda j: w.at[j, :, :, lanes[0]])
    w_y1 = RingGather(links, yy, y_up, y_down, lambda j: w.at[:, j, :, lanes[1]])
    upper, lower = pl.ds(0, 192), pl.ds(192, 192)
    y_y0 = RingGather(links, yy, y_up, y_down, lambda j: y.at[z, upper, lane_block(j)])
    y_z1 = RingGather(links, z, z_up, z_down, lambda j: y.at[j, lower, lane_block(yy)])
    y_z0 = RingGather(links, z, z_up, z_down, lambda j: y.at[j, upper])
    y_y1 = RingGather(links, yy, y_up, y_down, lambda j: y.at[:, lower, lane_block(j)])
    pan_x = RingGather(links, x, x_up, x_down, lambda j: pan.at[j, :, half_columns(k)])

    wc[0] = sum_z0.finish()
    wc[1] = sum_y1.finish()
    sum_y0.start()
    sum_z1.start()

    for copy in q4 + p4:
        copy.wait_recv()
    own_s = sf.at[k]
    swap_s = links.copy(own_s, own_s, sibling)
    pan_x.own()
    sum_y0.near()
    sum_z1.near()
    swap_s.wait_recv()
    for v in range(2):
        for j in range(2):
            xs[:, 256 * v + 128 * j : 256 * v + 128 * j + 128] = sf[:, v, :, :, j].transpose(1, 0, 2, 3, 4).reshape(512, 128)

    swaps = []

    def start_columns():
        moved.wait_recv()
        y_y0.own()
        y_z1.own()

    def start_weights():
        w[z, yy, :, 0:256] = sum_y0.finish()
        w[z, yy, :, 256:512] = sum_z1.finish()
        w_y0.own()
        w_z1.own()

    def swap_panel():
        pan_x.finish()
        for n in range(4):
            part = pan.at[(x + n) % 4, :, half_columns(k)]
            swaps.append(links.copy(part, part, sibling))

    def steps(*todo):
        def run():
            for step in todo:
                step()

        return run

    places = [
        steps(start_columns),
        steps(start_weights),
        steps(),
        steps(y_y0.forward, y_z1.forward, pan_x.forward),
        steps(w_y0.forward, w_z1.forward),
        steps(),
        steps(y_y0.finish, y_z0.own, y_z1.finish, y_y1.own),
        steps(w_y0.finish, w_z1.finish, w_z0.own, w_y1.own),
        steps(swap_panel),
        steps(),
        steps(),
        steps(),
        steps(y_z0.forward, y_y1.forward),
        steps(),
        steps(w_z0.forward, w_y1.forward),
    ]
    places += [steps()] * (16 - len(places))
    for n in range(4):
        invert_block(xs, n, places[4 * n : 4 * n + 4])
    for copy in swaps:
        copy.wait_recv()
    ah, al = split2(xs[...])
    bh, bl = split2(pan[...].reshape(512, 768))
    hi, lo = split2(dot(jnp.concatenate([al, ah, ah], axis=1), jnp.concatenate([bh, bl, bh], axis=0), NN))
    mv[0:512, :] = hi
    mv[512:1024, :] = lo
    mv[1024:1536, :] = hi
    w_z0.finish()
    w_y1.finish()
    y_z0.finish()
    y_y1.finish()
    for copy in h_copies + w_copies:
        copy.wait()
    links.drain()


COPIES = 180


def solve(t, wt, sc, hinverse, weights):
    return pl.pallas_call(
        solve_kernel,
        out_shape=[
            jax.ShapeDtypeStruct((1536, 768), B),
            jax.ShapeDtypeStruct((4, 384, 512), F),
            jax.ShapeDtypeStruct((4, 4, 48, 512), F),
            jax.ShapeDtypeStruct((1536, 768), F),
            jax.ShapeDtypeStruct((768, 768), F),
        ],
        in_specs=[VMEM] * 3 + [HBM] * 2,
        out_specs=[VMEM] * 5,
        scratch_shapes=[
            pltpu.VMEM((4, 128, 384), F),
            pltpu.VMEM((2, 64, 384), F),
            pltpu.VMEM((2, 128, 384), F),
            pltpu.VMEM((2, 4, 48, 256), F),
            pltpu.VMEM((4, 2, 48, 256), F),
            pltpu.VMEM((4, 4, 48, 256), F),
            pltpu.VMEM((4, 24, 256), F),
            pltpu.VMEM((4, 48, 256), F),
            pltpu.VMEM((2, 4, 8, 2, 8, 128), F),
            pltpu.VMEM((3, 8, 2, 8, 128), F),
            pltpu.VMEM((15, 4, 8, 128), F),
            pltpu.VMEM((8, 2, 8, 128), F),
            pltpu.VMEM((4, 8, 128), F),
            pltpu.VMEM((15, 8, 128), F),
            pltpu.VMEM((3, 8, 128), F),
            pltpu.VMEM((2, 2, 4, 8, 2, 8, 128), F),
            pltpu.VMEM((4, 128, 768), F),
            pltpu.VMEM((384, 128), F),
            pltpu.VMEM((512, 512), F),
            pltpu.SemaphoreType.DMA((COPIES,)),
            pltpu.SemaphoreType.DMA((COPIES,)),
            pltpu.SemaphoreType.DMA((21,)),
        ],
        compiler_params=pltpu.CompilerParams(vmem_limit_bytes=32 * MIB, collective_id=0, has_side_effects=True),
        name="solve",
    )(t.reshape(4, 128, 768), wt.reshape(4, 4, 48, 512), sc, hinverse, weights)


def update_kernel(hv, wv, p_ref, mm, yv, wt, ho_hbm, wo_hbm, hn, wn, osem):
    col = lax.axis_index("col")
    cols = local_place(p_ref, 16, col)
    lane = lax.broadcasted_iota(jnp.int32, cols.shape, 1)
    hit = [jnp.max((cols == lane + 128 * q).astype(F), axis=0, keepdims=True) for q in range(6)]
    pruned_here = jnp.concatenate(hit, axis=1) > 0.5
    outs = []

    def put(src, dst):
        copy = pltpu.make_async_copy(src, dst, osem.at[len(outs)])
        copy.start()
        outs.append(copy)

    def product(left):
        hi, lo = split2(left)
        return dot(jnp.concatenate([hi, hi, lo], axis=1), mm[...], NN)

    for hi in range(2):
        change = product(yv[2 - 2 * hi : 4 - 2 * hi].reshape(768, 512))
        for n in range(3):
            a = 2 * n + hi
            here = slice(256 * a, 256 * a + 256)
            hn[here, :] = hv[here, :] - change[256 * n : 256 * n + 256, :]
            for b in range(3):
                put(hn.at[pl.ds(256 * a, 256), pl.ds(256 * b, 256)], ho_hbm.at[a, 0, :, b, 0, :])
    wn[...] = jnp.where(pruned_here, 0.0, wv[...] - product(wt[...]))
    for b in range(3):
        put(wn.at[:, pl.ds(256 * b, 256)], wo_hbm.at[:, b, 0, :])
    for copy in outs:
        copy.wait()


def update(hinverse, pruned, weights, hv, wv, m, y, wt):
    return pl.pallas_call(
        update_kernel,
        out_shape=[jax.ShapeDtypeStruct(hinverse.shape, F), jax.ShapeDtypeStruct(weights.shape, F)],
        in_specs=[VMEM] * 6,
        out_specs=[HBM, HBM],
        scratch_shapes=[
            pltpu.VMEM((1536, 768), F),
            pltpu.VMEM((768, 768), F),
            pltpu.SemaphoreType.DMA((21,)),
        ],
        compiler_params=pltpu.CompilerParams(vmem_limit_bytes=36 * MIB),
        name="update",
    )(hv, wv, pruned, m, y, wt)


def per_device(hinverse, pruned, weights):
    t, wt, sc = gather(hinverse, pruned, weights)
    m, y, w, hv, wv = solve(t, wt, sc, hinverse, weights)
    return update(hinverse, pruned, weights, hv, wv, m, y, w.reshape(768, 512))


def solution(mesh):
    placed = (P(None, "row", None, None, "col", None), P(), P("row", None, "col", None))
    return jax.shard_map(
        per_device,
        mesh=mesh,
        in_specs=placed,
        out_specs=(P(None, "row", None, None, "col", None), P("row", None, "col", None)),
        check_vma=False,
    )
```
